512 devices in a mesh: tile: 128 (over x, z, core), ch: 4 (over y).
Axes of the slice: x: 4, y: 4, z: 16, core: 2. Of those that a mesh axis runs over, the one named last changes fastest.
Arguments:
- phases: float32 [32, 1024, 16, 128], P('ch', 'tile'), may hold values from 0 to 1
- node_temp: float32 [32768, 128], P('tile'), may hold values from -6 to 6
- column_nodes: int32 [16384], P('tile'), may hold values from 0 to 32767, as said below
- grain_ids: int32 [128, 32], P('tile'), may hold values from 0 to 4095, as said below
- grain_angle: float32 [4096], replicated, may hold values from -3.140625 to 3.140625
- grain_melt: float32 [4096], replicated, may hold values from -1 to 1
- heat_owner: int32 [2048, 1], P('tile'), may hold values from 0 to 127, as said below
- heat_local: int32 [2048], P('tile'), may hold values from 0 to 255
Outputs:
- phases_out: float32 [32, 1024, 16, 128], P('ch', 'tile')
- temp_out: float32 [32768, 128], P('tile')
The draws below stay inside these ranges and needn't reach their ends.
Inputs may be any that keep to these rules, and one draw needn't show every extreme that they name: `column_nodes`: node ids; of the 128 columns of one tile at most 2 take nodes of one owner (id // 256), and exactly 2 take nodes of that tile's own index. `grain_ids`: the 32 ids of a row are distinct. `heat_owner`: A row of tile t names an owner (t + d) mod 128 with d from -3 to 3; in the rows of one tile index no owner is named more than 4 times, and one owner exactly 4 times.
All inputs are finite; a program needn't handle non-finite values.
Results may differ from the reference program's by a relative error of at most 0.0003.
Values may be sent and summed in bfloat16 or wider, within the bound.
A program may use at most 64 MiB of HBM per device.

```python
import jax
import jax.numpy as jnp
from jax import lax

P_SIZE = 32
GRAINS = 4096
CX = 8
CY = 16
NZ = 128
NODE_DEV = 256
STEPS = 2
NX = 1024
NODES = 32768
COLS = 128
COLS_ALL = 16384
CAP = 2
POOL_DEV = 16
POOL_ALL = 2048
HCAP = 4
N_TILE = 128


def draw_column_nodes(key, part):
    key = jax.random.fold_in(key, 11)

    def one_tile(tile_key, tile):
        key_pool, key_order, key_local = jax.random.split(tile_key, 3)
        pool = jnp.arange((N_TILE - 1) * CAP, dtype=jnp.int32) // CAP
        others = (tile + 1 + jax.random.permutation(key_pool, pool)) % N_TILE
        owners = jnp.concatenate([jnp.full((CAP,), 1, jnp.int32) * tile, others[:COLS - CAP]])
        owners = jax.random.permutation(key_order, owners)
        local = jax.random.randint(key_local, (COLS,), 0, NODE_DEV, dtype=jnp.int32)
        return owners * NODE_DEV + local
    tiles = jnp.arange(N_TILE, dtype=jnp.int32)
    keys = jax.random.split(key, N_TILE)
    return jax.vmap(one_tile)(keys, tiles).reshape(COLS_ALL).astype(jnp.int32)


def draw_grain_ids(key, part):
    key = jax.random.fold_in(key, 23)
    keys = jax.random.split(key, N_TILE)
    return jax.vmap(lambda tile_key: jax.random.permutation(tile_key, GRAINS)[:P_SIZE])(keys).astype(jnp.int32)


def draw_heat_owner(key, part):
    key = jax.random.fold_in(key, 37)

    def one_tile(tile_key, tile):
        key_full, key_pool, key_order = jax.random.split(tile_key, 3)
        busiest = jax.random.randint(key_full, (), 0, 7, dtype=jnp.int32)
        pool = jnp.arange(6 * HCAP, dtype=jnp.int32) // HCAP
        others = (busiest + 1 + jax.random.permutation(key_pool, pool)) % 7
        picks = jnp.concatenate([jnp.full((HCAP,), 1, jnp.int32) * busiest, others[:POOL_DEV - HCAP]])
        picks = jax.random.permutation(key_order, picks)
        return (tile + picks - 3 + N_TILE) % N_TILE
    tiles = jnp.arange(N_TILE, dtype=jnp.int32)
    keys = jax.random.split(key, N_TILE)
    return jax.vmap(one_tile)(keys, tiles).reshape(POOL_ALL, 1).astype(jnp.int32)


def with_ends(entries, own_key, low, largest):
    longest = entries.shape.index(max(entries.shape))
    spots = []
    for shift in (0, 1):
        where = [jax.random.randint(jax.random.fold_in(own_key, axis), (), 0, length) for axis, length in enumerate(entries.shape)]
        where[longest] = (where[longest] + shift) % entries.shape[longest]
        spots.append(tuple(where))
    return entries.at[spots[0]].set(low).at[spots[1]].set(largest)


def shard_levels(stream_key, extent, shards, low, top_value):
    def one(axis_at, parts):
        draws = jax.random.uniform(jax.random.fold_in(jax.random.fold_in(stream_key, 6), axis_at), (parts,), jnp.float32, low / len(shards), top_value / len(shards))
        return jnp.repeat(jnp.exp(draws), extent[axis_at] // parts).reshape((-1,) + (1,) * (len(extent) - axis_at - 1))

    loudness = one(*shards[0])
    for cut in shards[1:]:
        loudness = loudness * one(*cut)
    return loudness


def bell_draw(rng, shape, scale, most, pieces=(), kind=jnp.bfloat16):
    result = scale * jax.random.normal(rng, shape, jnp.float32)
    if pieces:
        result = result * shard_levels(rng, shape, pieces, -0.22, 0.18)
    return jnp.clip(result, -most, most).astype(kind)


def setup_inputs(seed: int = 0) -> dict:
    key_of = jax.random.split(jax.random.key(seed), 9)
    phases = jnp.clip(1.0 * jax.random.uniform(key_of[0], (P_SIZE, NX, CY, NZ), jnp.float32) ** shard_levels(key_of[0], (P_SIZE, NX, CY, NZ), ((0, 4), (1, 128)), -0.2, 0.2), 0.0, 1.0)
    node_temp = bell_draw(key_of[1], (NODES, NZ), 1.0, 6.0, ((0, 128),), jnp.float32)
    column_nodes = draw_column_nodes(jax.random.fold_in(key_of[8], 71), 0)
    grain_ids = draw_grain_ids(jax.random.fold_in(key_of[8], 71), 0)
    grain_angle = jnp.clip(jax.random.uniform(key_of[4], (GRAINS,), jnp.float32, -3.140625, 3.140625), -3.140625, 3.140625)
    grain_melt = jnp.clip(jax.random.uniform(key_of[5], (GRAINS,), jnp.float32, -1.0, 1.0), -1.0, 1.0)
    heat_owner = draw_heat_owner(jax.random.fold_in(key_of[8], 71), 0)
    heat_local = with_ends(jax.random.randint(key_of[7], (POOL_ALL,), 0, NODE_DEV), jax.random.fold_in(key_of[7], 1), 0, NODE_DEV - 1).astype(jnp.int32)
    return dict(phases=phases, node_temp=node_temp, column_nodes=column_nodes, grain_ids=grain_ids, grain_angle=grain_angle, grain_melt=grain_melt, heat_owner=heat_owner, heat_local=heat_local)


time_step = 0.1
stiffness = 1.0
interface_energy = 1.0
drive_gain = 3.0
heat_gain = 0.5
depth_diffusion = 0.2


def neighbours(values, axis):
    length = values.shape[axis]
    widths = [(0, 0)] * values.ndim
    widths[axis] = (1, 1)
    padded = jnp.pad(values, widths)
    return lax.slice_in_dim(padded, 2, length + 2, axis=axis) + lax.slice_in_dim(padded, 0, length, axis=axis)


def sideways(values):
    return values[:, 2:] + values[:, :-2]


def middle(values):
    return values[:, 1:-1]


def laplacian(padded):
    along_y = neighbours(padded, 2)
    along_z = neighbours(padded, 3)
    along_yz = neighbours(along_y, 3)
    faces = sideways(padded) + middle(along_y) + middle(along_z)
    edges = sideways(along_y) + sideways(along_z) + middle(along_yz)
    corners = sideways(along_yz)
    return (6.0 * faces + 3.0 * edges + 2.0 * corners - 88.0 * middle(padded)) / 26.0


def coupling(angles):
    spread = angles[..., :, None] - angles[..., None, :]
    count = angles.shape[-1]
    off_diagonal = 1.0 - jnp.eye(count, dtype=jnp.float32)
    return (interface_energy / count * (0.3 + jnp.abs(jnp.sin(spread))) * off_diagonal).astype(jnp.bfloat16)


def advance(padded, mixing, cell_temp, melts):
    current = middle(padded)
    drive = -drive_gain * (cell_temp[None] - melts[:, None, None, None]) * current * (1.0 - current)
    return current + time_step * ((stiffness * laplacian(padded) - mixing) + drive)


def pooled_heat(updated, current):
    latent = jnp.sum(updated - current, axis=0)
    planes, across, depth = latent.shape
    return latent.reshape(planes, across // 8, 8, depth).sum(axis=2).reshape(planes * (across // 8), depth)


def conduct(node_temp, heat):
    edged = jnp.pad(node_temp, ((0, 0), (1, 1)), mode="edge")
    return node_temp + heat_gain * heat + depth_diffusion * (edged[:, 2:] - 2.0 * node_temp + edged[:, :-2])


def reference(phases, node_temp, column_nodes, grain_ids, grain_angle, grain_melt, heat_owner, heat_local):
    weights = coupling(grain_angle[grain_ids])
    melts = grain_melt[grain_ids]
    targets = heat_owner[:, 0] * NODE_DEV + heat_local
    tiles = jnp.arange(N_TILE, dtype=jnp.int32)
    for repeat in range(STEPS):
        cell_temp = node_temp[column_nodes].reshape(NX, CY, NZ)
        padded_all = jnp.pad(phases, ((0, 0), (1, 1), (0, 0), (0, 0)))

        def one_tile(tile):
            start = (tile * CX).astype(jnp.int32)
            padded = lax.dynamic_slice_in_dim(padded_all, start, CX + 2, 1)
            current = middle(padded)
            rounded = lax.optimization_barrier(current.astype(jnp.bfloat16)).astype(jnp.float32)
            mixing = jnp.einsum("ij,jxyz->ixyz", weights[tile].astype(jnp.float32), rounded)
            temp_tile = lax.dynamic_slice_in_dim(cell_temp, start, CX, 0)
            updated = advance(padded, mixing, temp_tile, melts[tile])
            return updated, pooled_heat(updated, current)

        updated, pooled = lax.map(one_tile, tiles)
        phases = jnp.moveaxis(updated, 1, 0).reshape(P_SIZE, NX, CY, NZ)
        heat = jnp.zeros((NODES, NZ), jnp.float32).at[targets].add(pooled.reshape(POOL_ALL, NZ))
        node_temp = conduct(node_temp, heat)
    return phases, node_temp
```

```python
import functools

import jax
import jax.numpy as jnp
from jax import lax
from jax.experimental import pallas as pl
from jax.experimental.pallas import tpu as pltpu
from jax.sharding import PartitionSpec as P

STEPS = 2
MESH = pl.DeviceIdType.MESH
F32 = jnp.float32
BF16 = jnp.bfloat16

time_step = 0.1
interface_energy = 1.0
drive_gain = 3.0
heat_gain = 0.5
depth_diffusion = 0.2

TILES = 128
GROUPS = 4
BLOCK = TILES // GROUPS
SLOTS = 2
REACH = 3
NEAR = 2 * REACH + 1
HEAT_SLOTS = 4
CH = 8
SLOT_ALL = 32
PX = 8
PY = 16
NZ = 128
COLS = PX * PY
NODES = 256
POOL = 16
FAR = BLOCK * SLOTS
HEAT_ROWS = NEAR * HEAT_SLOTS
HEAT_PAD = 32


def iota(shape, dim):
    return lax.broadcasted_iota(jnp.int32, shape, dim)


def dot(a, b):
    return jnp.dot(a, b, preferred_element_type=F32)


def thirds(value):
    high = value.astype(BF16)
    rest = value - high.astype(F32)
    mid = rest.astype(BF16)
    low = (rest - mid.astype(F32)).astype(BF16)
    return high, mid, low


def pick(onehot, value):
    high, mid, low = thirds(value)
    return dot(onehot, high) + (dot(onehot, mid) + dot(onehot, low))


def beside(values):
    rows, lanes = values.shape
    lane = iota((rows, lanes), 1)
    up = jnp.where(lane == lanes - 1, 0.0, pltpu.roll(values, lanes - 1, 1))
    down = jnp.where(lane == 0, 0.0, pltpu.roll(values, 1, 1))
    return up + down


def across(values):
    rows, lanes = values.shape
    place = iota((rows, lanes), 0) % PY
    up = jnp.where(place == PY - 1, 0.0, pltpu.roll(values, rows - 1, 0))
    down = jnp.where(place == 0, 0.0, pltpu.roll(values, 1, 0))
    return up + down


def laplacian(padded):
    flat = padded.reshape((PX + 2) * PY, NZ)
    along_y = across(flat)
    inner = (6.0 * along_y - 88.0 * flat) + beside(6.0 * flat + 3.0 * along_y)
    outer = (6.0 * flat + 3.0 * along_y) + beside(3.0 * flat + 2.0 * along_y)
    total = inner[PY:-PY] + (outer[2 * PY :] + outer[: -2 * PY])
    return total * (1.0 / 26.0)


def conduct(rows):
    lane = iota(rows.shape, 1)
    up = jnp.where(lane == NZ - 1, rows, pltpu.roll(rows, NZ - 1, 1))
    down = jnp.where(lane == 0, rows, pltpu.roll(rows, 1, 1))
    return rows + depth_diffusion * (up - 2.0 * rows + down)


def kernel(
    phases_hbm, temp_hbm, columns_hbm, grains_hbm, angle_hbm, melt_hbm, owner_hbm, local_hbm,
    phases_out, temp_out,
    cells, cells2, static, static2, mixed, gathered, gathered2,
    temp, columns, grains, angles, melts, owners, locals_,
    req_out, req_in, rows_out, rows_in, rows_out2, rows_in2, share, share2,
    heat_out, heat_in, heat_out2, heat_in2, target_out, target_in,
    own_v, all_v, all_v2, flat, heat_flat, final_temp,
    load_sem, send_sem, recv_sem,
):
    tile = lax.axis_index("tile")
    group = lax.axis_index("ch")
    block = tile // BLOCK
    place = tile % BLOCK
    partner = (group + GROUPS - block) % GROUPS
    inside = partner == block

    def far_device(index):
        return {"tile": partner * BLOCK + index, "ch": group}

    def near_device(offset, turn):
        return {"tile": (tile + offset + (TILES - REACH)) % TILES, "ch": (group + turn) % GROUPS}

    barrier = pltpu.get_barrier_semaphore()

    def greet_far(index, _):
        @pl.when(jnp.logical_or(jnp.logical_not(inside), index != place))
        def _():
            pl.semaphore_signal(barrier, inc=1, device_id=far_device(index), device_id_type=MESH)

        return 0

    def greet_near(index, _):
        offset, turn = index // GROUPS, index % GROUPS

        @pl.when(jnp.logical_or(offset != REACH, turn != 0))
        def _():
            pl.semaphore_signal(
                barrier, inc=1, device_id=near_device(offset, turn), device_id_type=MESH
            )

        return 0

    lax.fori_loop(0, BLOCK, greet_far, 0)
    lax.fori_loop(0, NEAR * GROUPS, greet_near, 0)

    loads = [
        pltpu.make_async_copy(phases_hbm, cells.at[:, pl.ds(1, PX)], load_sem.at[0]),
        pltpu.make_async_copy(temp_hbm, temp, load_sem.at[1]),
        pltpu.make_async_copy(columns_hbm, columns, load_sem.at[2]),
        pltpu.make_async_copy(grains_hbm, grains, load_sem.at[3]),
        pltpu.make_async_copy(angle_hbm, angles, load_sem.at[4]),
        pltpu.make_async_copy(melt_hbm, melts, load_sem.at[5]),
        pltpu.make_async_copy(owner_hbm, owners, load_sem.at[6]),
        pltpu.make_async_copy(local_hbm, locals_, load_sem.at[7]),
    ]
    for load in loads:
        load.start()
    for load in loads:
        load.wait()

    wanted = jnp.broadcast_to(columns[...].astype(F32), (COLS, COLS))
    wanted_down = wanted.T
    wanted_i = wanted.astype(jnp.int32)
    wanted_down_i = wanted_down.astype(jnp.int32)
    owner_over = wanted_i // NODES
    owner_down = wanted_down_i // NODES
    local_down = (wanted_down_i % NODES).astype(F32)
    down, over = iota((COLS, COLS), 0), iota((COLS, COLS), 1)
    same = owner_over == owner_down
    slot_over = jnp.sum(jnp.where(same & (down < over), 1.0, 0.0), axis=0, keepdims=True)
    slot_down = jnp.sum(jnp.where(same & (over < down), 1.0, 0.0), axis=1, keepdims=True)
    key_over = owner_over[:1] * SLOTS + slot_over.astype(jnp.int32)
    key_down = owner_down[:, :1] * SLOTS + slot_down.astype(jnp.int32)
    ask = jnp.where(iota((FAR, COLS), 0) + partner * FAR == key_over, 1.0, 0.0).astype(BF16)
    flat[pl.ds(0, FAR), :] = dot(ask, local_down.astype(BF16))
    for index in range(BLOCK):
        req_out[index] = flat[pl.ds(index * SLOTS, SLOTS), :]
    key_lane = iota((COLS, FAR), 1)
    take_own = jnp.where(key_lane + partner * FAR == key_down, 1.0, 0.0).astype(BF16)
    lane_all = iota((COLS, GROUPS * FAR), 1)
    lane_block = (lane_all // FAR + GROUPS - block) % GROUPS
    take_all = jnp.where(
        lane_block * FAR + lane_all % FAR == key_down, 1.0, 0.0
    ).astype(BF16)

    row_down, lane = iota((POOL, COLS), 0), iota((POOL, COLS), 1)
    off_down = jnp.zeros((POOL, COLS), jnp.int32)
    off_over = jnp.zeros((POOL, COLS), jnp.int32)
    local_rows = jnp.zeros((POOL, NZ), jnp.int32)
    for row in range(POOL):
        off = (owners[row] - tile + (REACH + TILES)) % TILES
        off_down = jnp.where(row_down == row, off, off_down)
        off_over = jnp.where(lane // 8 == row, off, off_over)
        local_rows = jnp.where(row_down == row, locals_[row], local_rows)
    earlier = jnp.where((off_down == off_over) & (row_down < lane // 8), 1.0, 0.0)
    heat_slot = jnp.sum(earlier, axis=0, keepdims=True).astype(jnp.int32)
    heat_key = off_over[:1] * HEAT_SLOTS + heat_slot
    spread = iota((HEAT_PAD, COLS), 0) == heat_key
    pool_pick = jnp.where(spread, 1.0, 0.0).astype(BF16)
    row_of = jnp.where(iota((COLS, POOL), 0) == 8 * iota((COLS, POOL), 1), 1.0, 0.0).astype(BF16)
    row_pick = dot(pool_pick, row_of).astype(BF16)
    flat[pl.ds(0, HEAT_PAD), :] = dot(row_pick, local_rows.astype(F32).astype(BF16))
    for offset in range(NEAR):
        target_out[offset] = flat[pl.ds(offset * HEAT_SLOTS, HEAT_SLOTS), :]

    def first_look(channel, total):
        now = cells[channel, pl.ds(1, PX)]
        gathered[group, channel] = now.astype(BF16)
        return total + (now - now * now)

    total = lax.fori_loop(0, CH, first_look, jnp.zeros((PX, PY, NZ), F32))
    total = (time_step * drive_gain) * total.reshape(COLS, NZ)
    own_v[0] = total
    all_v[0] = total

    pl.semaphore_wait(
        barrier, NEAR * GROUPS - 1 + jnp.where(inside, BLOCK - 1, BLOCK).astype(jnp.int32)
    )

    def far_copy(source, target, index, number):
        return pltpu.make_async_remote_copy(
            src_ref=source.at[index],
            dst_ref=target.at[place],
            send_sem=send_sem.at[number],
            recv_sem=recv_sem.at[number],
            device_id=far_device(index),
            device_id_type=MESH,
        )

    def far_send(source, target, number):
        def one(index, _):
            @pl.when(jnp.logical_or(jnp.logical_not(inside), index != place))
            def _():
                far_copy(source, target, index, number).start()

            return 0

        lax.fori_loop(0, BLOCK, one, 0)

        @pl.when(inside)
        def _():
            target[place] = source[place]

    def far_done(buffer, sem, number):
        @pl.when(inside)
        def _():
            part = buffer.at[pl.ds(0, BLOCK - 1)]
            pltpu.make_async_copy(part, part, sem.at[number]).wait()

        @pl.when(jnp.logical_not(inside))
        def _():
            pltpu.make_async_copy(buffer, buffer, sem.at[number]).wait()

    def heat_send(source, target, number):
        def one(index, _):
            offset, turn = index // GROUPS, index % GROUPS

            @pl.when(jnp.logical_or(offset != REACH, turn != 0))
            def _():
                pltpu.make_async_remote_copy(
                    src_ref=source.at[offset],
                    dst_ref=target.at[offset * GROUPS + group],
                    send_sem=send_sem.at[number],
                    recv_sem=recv_sem.at[number],
                    device_id=near_device(offset, turn),
                    device_id_type=MESH,
                ).start()

            return 0

        lax.fori_loop(0, NEAR * GROUPS, one, 0)
        target[REACH * GROUPS + group] = source[REACH]

    def heat_done(buffer, sem, number):
        part = buffer.at[pl.ds(0, NEAR * GROUPS - 1)]
        pltpu.make_async_copy(part, part, sem.at[number]).wait()

    def target_send(number):
        def one(offset, _):
            @pl.when(offset != REACH)
            def _():
                pltpu.make_async_remote_copy(
                    src_ref=target_out.at[offset],
                    dst_ref=target_in.at[offset],
                    send_sem=send_sem.at[number],
                    recv_sem=recv_sem.at[number],
                    device_id=near_device(offset, 0),
                    device_id_type=MESH,
                ).start()

            return 0

        lax.fori_loop(0, NEAR, one, 0)
        target_in[REACH] = target_out[REACH]

    def target_done(buffer, sem, number):
        part = buffer.at[pl.ds(0, NEAR - 1)]
        pltpu.make_async_copy(part, part, sem.at[number]).wait()

    def group_copies(source_of, target_of, number):
        return [
            pltpu.make_async_remote_copy(
                src_ref=source_of(turn),
                dst_ref=target_of(turn),
                send_sem=send_sem.at[number + turn],
                recv_sem=recv_sem.at[number + turn],
                device_id=near_device(REACH, turn),
                device_id_type=MESH,
            )
            for turn in range(1, GROUPS)
        ]

    def halo_copies(buffer, number):
        return [
            pltpu.make_async_remote_copy(
                src_ref=buffer.at[:, 1],
                dst_ref=buffer.at[:, PX + 1],
                send_sem=send_sem.at[number],
                recv_sem=recv_sem.at[number],
                device_id=near_device(REACH - 1, 0),
                device_id_type=MESH,
            ),
            pltpu.make_async_remote_copy(
                src_ref=buffer.at[:, PX],
                dst_ref=buffer.at[:, 0],
                send_sem=send_sem.at[number + 1],
                recv_sem=recv_sem.at[number + 1],
                device_id=near_device(REACH + 1, 0),
                device_id_type=MESH,
            ),
        ]

    REQ, ROWS, ROWS2, HEAT, HEAT2, TARGET = 0, 1, 2, 3, 4, 5
    HALO, HALO2 = 6, 8
    GATHER, GATHER2, SHARE, SHARE2, VEE, VEE2 = 10, 14, 18, 22, 26, 30

    far_send(req_out, req_in, REQ)
    target_send(TARGET)
    halos = halo_copies(cells, HALO)
    vees = group_copies(lambda turn: own_v.at[0], lambda turn: all_v.at[turn], VEE)
    gathers = group_copies(
        lambda turn: gathered.at[group], lambda turn: gathered.at[group], GATHER
    )
    for copy in halos + vees + gathers:
        copy.start()

    angle_down = jnp.zeros((SLOT_ALL, NZ), F32)
    angle_over = jnp.zeros((SLOT_ALL, NZ), F32)
    slot_row, slot_lane = iota((SLOT_ALL, NZ), 0), iota((SLOT_ALL, NZ), 1)
    for slot in range(SLOT_ALL):
        angle = angles[grains[slot]]
        angle_down = jnp.where(slot_row == slot, angle, angle_down)
        angle_over = jnp.where(slot_lane == slot, angle, angle_over)
    strength = interface_energy / SLOT_ALL * (0.3 + jnp.abs(jnp.sin(angle_down - angle_over)))
    strength = jnp.where((slot_row != slot_lane) & (slot_lane < SLOT_ALL), strength, 0.0)
    strength = strength.astype(BF16)
    column_sums = jnp.sum(strength.astype(F32), axis=0, keepdims=True)
    own_row = iota((COLS, SLOT_ALL), 0) // PY + group * CH
    choose = jnp.where(own_row == iota((COLS, SLOT_ALL), 1), 1.0, 0.0).astype(BF16)
    tall = dot(choose, strength).astype(BF16)
    wide_shape = (NZ, SLOT_ALL * PY)
    widen = jnp.where(iota(wide_shape, 0) == iota(wide_shape, 1) // PY, 1.0, 0.0).astype(BF16)
    weights = dot(tall, widen)
    weights = jnp.where(iota(wide_shape, 0) % PY == iota(wide_shape, 1) % PY, weights, 0.0)
    weights = weights.astype(BF16)

    def melt_of(channel):
        return melts[grains[group * CH + channel]]

    def sum_of(channel):
        lanes = iota((1, NZ), 1) == group * CH + channel
        return jnp.sum(jnp.where(lanes, column_sums, 0.0), axis=1, keepdims=True)

    def stencil(buffer, kept):
        @pl.when(tile == 0)
        def _():
            buffer[:, 0] = jnp.zeros((CH, PY, NZ), F32)

        @pl.when(tile == TILES - 1)
        def _():
            buffer[:, PX + 1] = jnp.zeros((CH, PY, NZ), F32)

        def one(channel, total):
            padded = buffer[channel]
            now = padded[1:-1].reshape(COLS, NZ)
            gain = time_step * laplacian(padded)
            gain = gain + (melt_of(channel) * (time_step * drive_gain)) * (now - now * now)
            kept[channel] = now + gain
            rounded = now.astype(BF16).astype(F32)
            return total + (gain - (time_step * sum_of(channel)) * rounded)

        return lax.fori_loop(0, CH, one, jnp.zeros((COLS, NZ), F32))

    def mix(buffer):
        for plane in range(PX):
            right = buffer[:, :, plane].reshape(SLOT_ALL * PY, NZ)
            mixed[:, plane] = dot(weights, right).reshape(CH, PY, NZ)

    for copy in halos:
        copy.wait_recv()
    own_u = stencil(cells, static)

    far_done(req_in, recv_sem, REQ)
    for index in range(BLOCK):
        flat[pl.ds(index * SLOTS, SLOTS), :] = req_in[index]
    asked = flat[pl.ds(0, FAR), :].astype(jnp.int32)
    asked = jnp.concatenate([asked, asked], axis=1)
    serve = jnp.where(asked == iota((FAR, NODES), 1), 1.0, 0.0).astype(BF16)

    def spread_rows(values, out):
        flat[pl.ds(0, FAR), :] = values
        for index in range(BLOCK):
            out[index] = flat[pl.ds(index * SLOTS, SLOTS), :]

    def collect_rows(buffer, kept):
        for index in range(BLOCK):
            kept[0, pl.ds(index * SLOTS, SLOTS), :] = buffer[index]

    spread_rows(pick(serve, temp[...]), rows_out)
    far_send(rows_out, rows_in, ROWS)

    target_done(target_in, recv_sem, TARGET)
    heat_flat[...] = jnp.full((HEAT_PAD, NZ), -1.0, F32)
    for offset in range(NEAR):
        heat_flat[pl.ds(offset * HEAT_SLOTS, HEAT_SLOTS), :] = target_in[offset]
    aims = heat_flat[...].astype(jnp.int32)
    aims = jnp.concatenate([aims, jnp.full((NZ - HEAT_PAD, NZ), -1, jnp.int32)], axis=0)
    low = jnp.where(aims == iota((NZ, NZ), 1), 1.0, 0.0).T
    high = jnp.where(aims == iota((NZ, NZ), 1) + NZ, 1.0, 0.0).T
    scatter = jnp.concatenate([low, high], axis=0)[:, :HEAT_PAD].astype(BF16)
    relay = dot(serve, scatter).astype(BF16)
    warm = conduct(temp[...])
    warm_rows = pick(serve, warm)
    heat_flat[...] = jnp.zeros((HEAT_PAD, NZ), F32)

    def arrived_heat(buffer):
        for offset in range(NEAR):
            parts = [buffer[offset * GROUPS + turn] for turn in range(GROUPS)]
            heat_flat[pl.ds(offset * HEAT_SLOTS, HEAT_SLOTS), :] = (parts[0] + parts[1]) + (
                parts[2] + parts[3]
            )
        return heat_flat[...]

    def send_heat(kept, own_part, vee, out, target, number):
        mine = pick(take_own, kept[0])
        amount = own_part - mine * vee
        flat[pl.ds(0, HEAT_PAD), :] = pick(pool_pick, amount)
        for offset in range(NEAR):
            out[offset] = flat[pl.ds(offset * HEAT_SLOTS, HEAT_SLOTS), :]
        heat_send(out, target, number)

    def share_copies(buffer, number):
        return group_copies(lambda turn: buffer.at[0], lambda turn: buffer.at[turn], number)

    turn_of = (group + GROUPS - lane_all // FAR) % GROUPS
    del turn_of
    take_turn = jnp.where(
        (((group + GROUPS - lane_all // FAR) % GROUPS + GROUPS - block) % GROUPS) * FAR
        + lane_all % FAR
        == key_down,
        1.0,
        0.0,
    ).astype(BF16)
    del take_all

    for copy in vees:
        copy.wait_recv()
    vee = (all_v[0] + all_v[1]) + (all_v[2] + all_v[3])

    far_done(rows_in, recv_sem, ROWS)
    collect_rows(rows_in, share)
    send_heat(share, own_u, vee, heat_out, heat_in, HEAT)
    shares = share_copies(share, SHARE)
    for copy in shares:
        copy.start()

    for copy in gathers:
        copy.wait_recv()
    mix(gathered)
    for copy in shares:
        copy.wait_recv()

    def all_rows(kept):
        return pick(take_turn, kept[...].reshape(GROUPS * FAR, NZ))

    cell_temp = all_rows(share)

    def update(channel, total):
        now = cells[channel, pl.ds(1, PX)].reshape(COLS, NZ)
        change = (time_step * drive_gain) * cell_temp * (now - now * now)
        mixing = mixed[channel].reshape(COLS, NZ)
        new = static[channel] - time_step * mixing - change
        shaped = new.reshape(PX, PY, NZ)
        cells2[channel, pl.ds(1, PX)] = shaped
        gathered2[group, channel] = shaped.astype(BF16)
        return total + (new - new * new)

    total = lax.fori_loop(0, CH, update, jnp.zeros((COLS, NZ), F32))
    total = (time_step * drive_gain) * total
    own_v[1] = total
    all_v2[0] = total
    halos2 = halo_copies(cells2, HALO2)
    vees2 = group_copies(lambda turn: own_v.at[1], lambda turn: all_v2.at[turn], VEE2)
    gathers2 = group_copies(
        lambda turn: gathered2.at[group], lambda turn: gathered2.at[group], GATHER2
    )
    for copy in halos2 + vees2 + gathers2:
        copy.start()

    heat_done(heat_in, recv_sem, HEAT)
    arrived = arrived_heat(heat_in)
    spread_rows(warm_rows + heat_gain * pick(relay, arrived), rows_out2)
    far_send(rows_out2, rows_in2, ROWS2)
    final_temp[...] = conduct(warm + heat_gain * pick(scatter, arrived))

    for copy in halos2:
        copy.wait_recv()
    own_u2 = stencil(cells2, static2)
    for copy in vees2:
        copy.wait_recv()
    vee2 = (all_v2[0] + all_v2[1]) + (all_v2[2] + all_v2[3])

    far_done(rows_in2, recv_sem, ROWS2)
    collect_rows(rows_in2, share2)
    send_heat(share2, own_u2, vee2, heat_out2, heat_in2, HEAT2)
    shares2 = share_copies(share2, SHARE2)
    for copy in shares2:
        copy.start()

    for copy in gathers2:
        copy.wait_recv()
    mix(gathered2)
    for copy in shares2:
        copy.wait_recv()
    cell_temp2 = all_rows(share2)

    def finish(channel, _):
        now = cells2[channel, pl.ds(1, PX)].reshape(COLS, NZ)
        change = (time_step * drive_gain) * cell_temp2 * (now - now * now)
        mixing = mixed[channel].reshape(COLS, NZ)
        new = static2[channel] - time_step * mixing - change
        static2[channel] = new
        return 0

    lax.fori_loop(0, CH, finish, 0)
    store = pltpu.make_async_copy(static2, phases_out, load_sem.at[0])
    store.start()

    heat_done(heat_in2, recv_sem, HEAT2)
    arrived = arrived_heat(heat_in2)
    final_temp[...] = final_temp[...] + heat_gain * pick(scatter, arrived)
    store_temp = pltpu.make_async_copy(final_temp, temp_out, load_sem.at[1])
    store_temp.start()

    far_done(req_out, send_sem, REQ)
    far_done(rows_out, send_sem, ROWS)
    far_done(rows_out2, send_sem, ROWS2)
    heat_done(heat_in, send_sem, HEAT)
    heat_done(heat_in2, send_sem, HEAT2)
    target_done(target_out, send_sem, TARGET)
    for copy in halos + vees + gathers + shares + halos2 + vees2 + gathers2 + shares2:
        copy.wait_send()
    store.wait()
    store_temp.wait()


def on_device(
    phases, node_temp, column_nodes, grain_ids, grain_angle, grain_melt, heat_owner, heat_local
):
    anywhere = pl.BlockSpec(memory_space=pl.ANY)
    vmem, smem = pltpu.VMEM, pltpu.SMEM
    gathered = vmem((GROUPS, CH, PX, PY, NZ), BF16)
    padded = vmem((CH, PX + 2, PY, NZ), F32)
    flat_cells = vmem((CH, COLS, NZ), F32)
    far_rows = vmem((BLOCK, SLOTS, NZ), F32)
    shared = vmem((GROUPS, FAR, NZ), F32)
    heat_out = vmem((NEAR, HEAT_SLOTS, NZ), F32)
    heat_in = vmem((NEAR * GROUPS, HEAT_SLOTS, NZ), F32)
    field = vmem((GROUPS, COLS, NZ), F32)
    new, temp = pl.pallas_call(
        kernel,
        out_shape=(
            jax.ShapeDtypeStruct((CH, COLS, NZ), F32),
            jax.ShapeDtypeStruct(node_temp.shape, F32),
        ),
        in_specs=[anywhere] * 8,
        out_specs=(anywhere, anywhere),
        scratch_shapes=[
            padded, padded, flat_cells, flat_cells, vmem((CH, PX, PY, NZ), F32), gathered, gathered,
            vmem((NODES, NZ), F32), vmem((1, COLS), jnp.int32), smem((SLOT_ALL,), jnp.int32),
            smem((grain_angle.shape[0],), F32), smem((grain_melt.shape[0],), F32),
            smem((POOL,), jnp.int32), smem((POOL,), jnp.int32),
            far_rows, far_rows, far_rows, far_rows, far_rows, far_rows, shared, shared,
            heat_out, heat_in, heat_out, heat_in, heat_out, heat_out,
            vmem((2, COLS, NZ), F32), field, field, vmem((FAR, NZ), F32), vmem((HEAT_PAD, NZ), F32),
            vmem((NODES, NZ), F32),
            pltpu.SemaphoreType.DMA((8,)),
            pltpu.SemaphoreType.DMA((34,)),
            pltpu.SemaphoreType.DMA((34,)),
        ],
        compiler_params=pltpu.CompilerParams(
            collective_id=0, has_side_effects=True, vmem_limit_bytes=56 << 20
        ),
        name="solidify",
    )(
        phases,
        node_temp,
        column_nodes.reshape(1, COLS),
        grain_ids.reshape(SLOT_ALL),
        grain_angle,
        grain_melt,
        heat_owner.reshape(POOL),
        heat_local,
    )
    return new.reshape(phases.shape), temp


def solution(mesh):
    placed = (
        P("ch", "tile", None, None),
        P("tile", None),
        P("tile"),
        P("tile", None),
        P(),
        P(),
        P("tile", None),
        P("tile"),
    )
    return jax.shard_map(
        on_device,
        mesh=mesh,
        in_specs=placed,
        out_specs=(P("ch", "tile", None, None), P("tile", None)),
        check_vma=False,
    )
```

```python
import functools

import jax
import jax.numpy as jnp
from jax import lax
from jax.experimental import pallas as pl
from jax.experimental.pallas import tpu as pltpu
from jax.sharding import PartitionSpec as P

STEPS = 2
MESH = pl.DeviceIdType.MESH
F32 = jnp.float32
BF16 = jnp.bfloat16

time_step = 0.1
interface_energy = 1.0
drive_gain = 3.0
heat_gain = 0.5
depth_diffusion = 0.2

TILES = 128
GROUPS = 4
BLOCK = TILES // GROUPS
SLOTS = 2
REACH = 3
NEAR = 2 * REACH + 1
HEAT_SLOTS = 4
CH = 8
SLOT_ALL = 32
PX = 8
PY = 16
NZ = 128
COLS = PX * PY
NODES = 256
POOL = 16
FAR = BLOCK * SLOTS
HEAT_ROWS = NEAR * HEAT_SLOTS
HEAT_PAD = 32
QUARTER = CH // 4


def iota(shape, dim):
    return lax.broadcasted_iota(jnp.int32, shape, dim)


def dot(a, b):
    return jnp.dot(a, b, preferred_element_type=F32)


def thirds(value):
    high = value.astype(BF16)
    rest = value - high.astype(F32)
    mid = rest.astype(BF16)
    low = (rest - mid.astype(F32)).astype(BF16)
    return high, mid, low


def stacked(value):
    return jnp.concatenate(thirds(value), axis=0)


def tripled(onehot):
    return jnp.concatenate([onehot, onehot, onehot], axis=1)


def beside(values):
    rows, lanes = values.shape
    lane = iota((rows, lanes), 1)
    up = jnp.where(lane == lanes - 1, 0.0, pltpu.roll(values, lanes - 1, 1))
    down = jnp.where(lane == 0, 0.0, pltpu.roll(values, 1, 1))
    return up + down


def across(values):
    rows, lanes = values.shape
    place = iota((rows, lanes), 0) % PY
    up = jnp.where(place == PY - 1, 0.0, pltpu.roll(values, rows - 1, 0))
    down = jnp.where(place == 0, 0.0, pltpu.roll(values, 1, 0))
    return up + down


def laplacian(padded):
    flat = padded.reshape((PX + 2) * PY, NZ)
    along_y = across(flat)
    inner = (6.0 * along_y - 88.0 * flat) + beside(6.0 * flat + 3.0 * along_y)
    outer = (6.0 * flat + 3.0 * along_y) + beside(3.0 * flat + 2.0 * along_y)
    total = inner[PY:-PY] + (outer[2 * PY :] + outer[: -2 * PY])
    return total * (1.0 / 26.0)


def conduct(rows):
    lane = iota(rows.shape, 1)
    up = jnp.where(lane == NZ - 1, rows, pltpu.roll(rows, NZ - 1, 1))
    down = jnp.where(lane == 0, rows, pltpu.roll(rows, 1, 1))
    return rows + depth_diffusion * (up - 2.0 * rows + down)


def kernel(
    phases_hbm, temp_hbm, columns_hbm, grains_hbm, angle_hbm, melt_hbm, owner_hbm, local_hbm,
    phases_out, temp_out,
    cells, cells2, static, static2, mixed, gathered, gathered2,
    temp, columns, grains, angles, melts, owners, locals_,
    req_out, req_in, rows_out, rows_in, rows_out2, rows_in2, share, share2,
    heat_out, heat_in, heat_out2, heat_in2, target_out, target_in,
    own_v, all_v, all_v2, flat, heat_flat, final_temp,
    load_sem, send_sem, recv_sem,
):
    tile = lax.axis_index("tile")
    group = lax.axis_index("ch")
    block = tile // BLOCK
    place = tile % BLOCK
    partner = (group + GROUPS - block) % GROUPS
    inside = partner == block

    first = partner * BLOCK
    near_tiles = [lax.rem(tile + (TILES + step - REACH), TILES) for step in range(NEAR)]
    groups = [group] + [lax.rem(group + turn, GROUPS) for turn in range(1, GROUPS)]
    near_order = [
        (offset, turn) for turn in (2, 1, 3, 0) for offset in (0, 6, 1, 5, 2, 4, 3)
    ][:-1]

    def far_index(number):
        half = (number + 1) // 2
        turn = jnp.where(number % 2 == 0, half, BLOCK - half)
        return lax.rem(place + BLOCK // 2 + turn, BLOCK)

    def far_device(index):
        return {"tile": first + index, "ch": group}

    def near_device(offset, turn):
        return {"tile": near_tiles[offset], "ch": groups[turn]}

    barrier = pltpu.get_barrier_semaphore()

    def greet_far(number, _):
        pl.semaphore_signal(
            barrier, inc=1, device_id=far_device(far_index(number)), device_id_type=MESH
        )
        return 0

    lax.fori_loop(0, BLOCK - 1, greet_far, 0)

    @pl.when(jnp.logical_not(inside))
    def _():
        greet_far(BLOCK - 1, 0)

    for offset, turn in near_order:
        pl.semaphore_signal(
            barrier, inc=1, device_id=near_device(offset, turn), device_id_type=MESH
        )

    loads = [
        pltpu.make_async_copy(phases_hbm, cells.at[:, pl.ds(1, PX)], load_sem.at[0]),
        pltpu.make_async_copy(temp_hbm, temp, load_sem.at[1]),
        pltpu.make_async_copy(columns_hbm, columns, load_sem.at[2]),
        pltpu.make_async_copy(grains_hbm, grains, load_sem.at[3]),
        pltpu.make_async_copy(angle_hbm, angles, load_sem.at[4]),
        pltpu.make_async_copy(melt_hbm, melts, load_sem.at[5]),
        pltpu.make_async_copy(owner_hbm, owners, load_sem.at[6]),
        pltpu.make_async_copy(local_hbm, locals_, load_sem.at[7]),
    ]
    for load in loads:
        load.start()
    for load in loads:
        load.wait()

    wanted = jnp.broadcast_to(columns[...].astype(F32), (COLS, COLS))
    wanted_down = wanted.T
    wanted_i = wanted.astype(jnp.int32)
    wanted_down_i = wanted_down.astype(jnp.int32)
    owner_over = wanted_i // NODES
    owner_down = wanted_down_i // NODES
    local_down = (wanted_down_i % NODES).astype(F32)
    down, over = iota((COLS, COLS), 0), iota((COLS, COLS), 1)
    same = owner_over == owner_down
    slot_over = jnp.sum(jnp.where(same & (down < over), 1.0, 0.0), axis=0, keepdims=True)
    slot_down = jnp.sum(jnp.where(same & (over < down), 1.0, 0.0), axis=1, keepdims=True)
    key_over = owner_over[:1] * SLOTS + slot_over.astype(jnp.int32)
    key_down = owner_down[:, :1] * SLOTS + slot_down.astype(jnp.int32)
    ask = jnp.where(iota((FAR, COLS), 0) + partner * FAR == key_over, 1.0, 0.0).astype(BF16)
    flat[pl.ds(0, FAR), :] = dot(ask, local_down.astype(BF16))
    for index in range(BLOCK):
        req_out[index] = flat[pl.ds(index * SLOTS, SLOTS), :]
    key_lane = iota((COLS, FAR), 1)
    take_own = jnp.where(key_lane + partner * FAR == key_down, 1.0, 0.0).astype(BF16)
    lane_all = iota((COLS, GROUPS * FAR), 1)
    lane_group = (group + GROUPS - lane_all // FAR) % GROUPS
    lane_block = (lane_group + GROUPS - block) % GROUPS
    take_turn = jnp.where(
        lane_block * FAR + lane_all % FAR == key_down, 1.0, 0.0
    ).astype(BF16)
    take_own, take_turn = tripled(take_own), tripled(take_turn)

    row_down, lane = iota((POOL, COLS), 0), iota((POOL, COLS), 1)
    off_down = jnp.zeros((POOL, COLS), jnp.int32)
    off_over = jnp.zeros((POOL, COLS), jnp.int32)
    local_rows = jnp.zeros((POOL, NZ), jnp.int32)
    for row in range(POOL):
        off = (owners[row] - tile + (REACH + TILES)) % TILES
        off_down = jnp.where(row_down == row, off, off_down)
        off_over = jnp.where(lane // 8 == row, off, off_over)
        local_rows = jnp.where(row_down == row, locals_[row], local_rows)
    earlier = jnp.where((off_down == off_over) & (row_down < lane // 8), 1.0, 0.0)
    heat_slot = jnp.sum(earlier, axis=0, keepdims=True).astype(jnp.int32)
    heat_key = off_over[:1] * HEAT_SLOTS + heat_slot
    spread = iota((HEAT_PAD, COLS), 0) == heat_key
    pool_pick = jnp.where(spread, 1.0, 0.0).astype(BF16)
    row_of = jnp.where(iota((COLS, POOL), 0) == 8 * iota((COLS, POOL), 1), 1.0, 0.0).astype(BF16)
    row_pick = dot(pool_pick, row_of).astype(BF16)
    pool_pick = tripled(pool_pick)
    flat[pl.ds(0, HEAT_PAD), :] = dot(row_pick, local_rows.astype(F32).astype(BF16))
    for offset in range(NEAR):
        target_out[offset] = flat[pl.ds(offset * HEAT_SLOTS, HEAT_SLOTS), :]

    def first_look(channel, total):
        now = cells[channel, pl.ds(1, PX)]
        gathered[group, channel] = now.astype(BF16)
        return total + (now - now * now)

    total = lax.fori_loop(0, CH, first_look, jnp.zeros((PX, PY, NZ), F32))
    total = (time_step * drive_gain) * total.reshape(COLS, NZ)
    own_v[0] = total
    all_v[0] = total

    warm = conduct(temp[...])
    cold_parts, warm_parts = stacked(temp[...]), stacked(warm)

    pl.semaphore_wait(
        barrier, NEAR * GROUPS - 1 + jnp.where(inside, BLOCK - 1, BLOCK).astype(jnp.int32)
    )

    def far_copy(source, target, index, number):
        return pltpu.make_async_remote_copy(
            src_ref=source.at[index],
            dst_ref=target.at[place],
            send_sem=send_sem.at[number],
            recv_sem=recv_sem.at[number],
            device_id=far_device(index),
            device_id_type=MESH,
        )

    def far_send(source, target, number):
        def one(order, _):
            far_copy(source, target, far_index(order), number).start()
            return 0

        lax.fori_loop(0, BLOCK - 1, one, 0)

        @pl.when(jnp.logical_not(inside))
        def _():
            one(BLOCK - 1, 0)

        @pl.when(inside)
        def _():
            target[place] = source[place]

    def far_done(buffer, sem, number):
        @pl.when(inside)
        def _():
            part = buffer.at[pl.ds(0, BLOCK - 1)]
            pltpu.make_async_copy(part, part, sem.at[number]).wait()

        @pl.when(jnp.logical_not(inside))
        def _():
            pltpu.make_async_copy(buffer, buffer, sem.at[number]).wait()

    def heat_send(source, target, number):
        for offset, turn in near_order:
            pltpu.make_async_remote_copy(
                src_ref=source.at[offset],
                dst_ref=target.at[offset * GROUPS + group],
                send_sem=send_sem.at[number],
                recv_sem=recv_sem.at[number],
                device_id=near_device(offset, turn),
                device_id_type=MESH,
            ).start()
        target[REACH * GROUPS + group] = source[REACH]

    def heat_done(buffer, sem, number):
        part = buffer.at[pl.ds(0, NEAR * GROUPS - 1)]
        pltpu.make_async_copy(part, part, sem.at[number]).wait()

    def target_send(number):
        for offset in (0, 6, 1, 5, 2, 4):
            pltpu.make_async_remote_copy(
                src_ref=target_out.at[offset],
                dst_ref=target_in.at[offset],
                send_sem=send_sem.at[number],
                recv_sem=recv_sem.at[number],
                device_id=near_device(offset, 0),
                device_id_type=MESH,
            ).start()
        target_in[REACH] = target_out[REACH]

    def target_done(buffer, sem, number):
        part = buffer.at[pl.ds(0, NEAR - 1)]
        pltpu.make_async_copy(part, part, sem.at[number]).wait()

    def group_copies(source_of, target_of, number):
        return [
            pltpu.make_async_remote_copy(
                src_ref=source_of(turn),
                dst_ref=target_of(turn),
                send_sem=send_sem.at[number + turn],
                recv_sem=recv_sem.at[number + turn],
                device_id=near_device(REACH, turn),
                device_id_type=MESH,
            )
            for turn in range(1, GROUPS)
        ]

    def ring_copies(buffer, number):
        def move(owner, part, turn, order):
            piece = buffer.at[owner, pl.ds(part * QUARTER, QUARTER)]
            return pltpu.make_async_remote_copy(
                src_ref=piece,
                dst_ref=piece,
                send_sem=send_sem.at[number + order],
                recv_sem=recv_sem.at[number + order],
                device_id=near_device(REACH, turn),
                device_id_type=MESH,
            )

        right = [move(group, part, 1, part) for part in (0, 1, 2, 3)]
        left = [move(group, part, 3, 4 + part) for part in (2, 3, 0, 1)]
        starts = [copy for pair in zip(right, left) for copy in pair]
        onward = []
        for step in range(2):
            onward.append(move(groups[3], step, 1, 8 + step))
            onward.append(move(groups[1], step + 2, 3, 10 + step))
        return starts, starts[:4], onward, starts[4:] + onward

    def halo_copies(buffer, number):
        return [
            pltpu.make_async_remote_copy(
                src_ref=buffer.at[:, 1],
                dst_ref=buffer.at[:, PX + 1],
                send_sem=send_sem.at[number],
                recv_sem=recv_sem.at[number],
                device_id=near_device(REACH - 1, 0),
                device_id_type=MESH,
            ),
            pltpu.make_async_remote_copy(
                src_ref=buffer.at[:, PX],
                dst_ref=buffer.at[:, 0],
                send_sem=send_sem.at[number + 1],
                recv_sem=recv_sem.at[number + 1],
                device_id=near_device(REACH + 1, 0),
                device_id_type=MESH,
            ),
        ]

    REQ, ROWS, ROWS2, HEAT, HEAT2, TARGET = 0, 1, 2, 3, 4, 5
    HALO, HALO2 = 6, 8
    GATHER, GATHER2, SHARE, SHARE2, VEE, VEE2 = 10, 14, 26, 30, 34, 38

    far_send(req_out, req_in, REQ)
    target_send(TARGET)
    halos = halo_copies(cells, HALO)
    vees = group_copies(lambda turn: own_v.at[0], lambda turn: all_v.at[turn], VEE)
    gathers = group_copies(
        lambda turn: gathered.at[group], lambda turn: gathered.at[group], GATHER
    )
    for copy in halos + vees + gathers:
        copy.start()

    angle_down = jnp.zeros((SLOT_ALL, NZ), F32)
    angle_over = jnp.zeros((SLOT_ALL, NZ), F32)
    slot_row, slot_lane = iota((SLOT_ALL, NZ), 0), iota((SLOT_ALL, NZ), 1)
    for slot in range(SLOT_ALL):
        angle = angles[grains[slot]]
        angle_down = jnp.where(slot_row == slot, angle, angle_down)
        angle_over = jnp.where(slot_lane == slot, angle, angle_over)
    strength = interface_energy / SLOT_ALL * (0.3 + jnp.abs(jnp.sin(angle_down - angle_over)))
    strength = jnp.where((slot_row != slot_lane) & (slot_lane < SLOT_ALL), strength, 0.0)
    strength = strength.astype(BF16)
    column_sums = jnp.sum(strength.astype(F32), axis=0, keepdims=True)
    own_row = iota((COLS, SLOT_ALL), 0) // PY + group * CH
    choose = jnp.where(own_row == iota((COLS, SLOT_ALL), 1), 1.0, 0.0).astype(BF16)
    tall = dot(choose, strength).astype(BF16)
    wide_shape = (NZ, SLOT_ALL * PY)
    widen = jnp.where(iota(wide_shape, 0) == iota(wide_shape, 1) // PY, 1.0, 0.0).astype(BF16)
    weights = dot(tall, widen)
    weights = jnp.where(iota(wide_shape, 0) % PY == iota(wide_shape, 1) % PY, weights, 0.0)
    weights = weights.astype(BF16)

    def melt_of(channel):
        return melts[grains[group * CH + channel]]

    def sum_of(channel):
        lanes = iota((1, NZ), 1) == group * CH + channel
        return jnp.sum(jnp.where(lanes, column_sums, 0.0), axis=1, keepdims=True)

    def stencil(buffer, kept):
        @pl.when(tile == 0)
        def _():
            buffer[:, 0] = jnp.zeros((CH, PY, NZ), F32)

        @pl.when(tile == TILES - 1)
        def _():
            buffer[:, PX + 1] = jnp.zeros((CH, PY, NZ), F32)

        def one(channel, total):
            padded = buffer[channel]
            now = padded[1:-1].reshape(COLS, NZ)
            gain = time_step * laplacian(padded)
            gain = gain + (melt_of(channel) * (time_step * drive_gain)) * (now - now * now)
            kept[channel] = now + gain
            rounded = now.astype(BF16).astype(F32)
            return total + (gain - (time_step * sum_of(channel)) * rounded)

        return lax.fori_loop(0, CH, one, jnp.zeros((COLS, NZ), F32))

    def mix(buffer):
        for plane in range(PX):
            right = buffer[:, :, plane].reshape(SLOT_ALL * PY, NZ)
            mixed[:, plane] = dot(weights, right).reshape(CH, PY, NZ)

    for copy in halos:
        copy.wait_recv()
    own_u = stencil(cells, static)

    far_done(req_in, recv_sem, REQ)
    for index in range(BLOCK):
        flat[pl.ds(index * SLOTS, SLOTS), :] = req_in[index]
    asked = flat[pl.ds(0, FAR), :].astype(jnp.int32)
    asked = jnp.concatenate([asked, asked], axis=1)
    serve = jnp.where(asked == iota((FAR, NODES), 1), 1.0, 0.0).astype(BF16)

    def spread_rows(values, out):
        flat[pl.ds(0, FAR), :] = values
        for index in range(BLOCK):
            out[index] = flat[pl.ds(index * SLOTS, SLOTS), :]

    def collect_rows(buffer, kept):
        for index in range(BLOCK):
            kept[0, pl.ds(index * SLOTS, SLOTS), :] = buffer[index]

    serve = tripled(serve)
    spread_rows(dot(serve, cold_parts), rows_out)
    far_send(rows_out, rows_in, ROWS)

    target_done(target_in, recv_sem, TARGET)
    heat_flat[...] = jnp.full((HEAT_PAD, NZ), -1.0, F32)
    for offset in range(NEAR):
        heat_flat[pl.ds(offset * HEAT_SLOTS, HEAT_SLOTS), :] = target_in[offset]
    aims = heat_flat[...].astype(jnp.int32)
    aims = jnp.concatenate([aims, jnp.full((NZ - HEAT_PAD, NZ), -1, jnp.int32)], axis=0)
    low = jnp.where(aims == iota((NZ, NZ), 1), 1.0, 0.0).T
    high = jnp.where(aims == iota((NZ, NZ), 1) + NZ, 1.0, 0.0).T
    scatter = jnp.concatenate([low, high], axis=0)[:, :HEAT_PAD].astype(BF16)
    relay = tripled(dot(serve[:, :NODES], scatter).astype(BF16))
    scatter = tripled(scatter)
    warm_rows = dot(serve, warm_parts)
    heat_flat[...] = jnp.zeros((HEAT_PAD, NZ), F32)

    def arrived_heat(buffer):
        for offset in range(NEAR):
            parts = [buffer[offset * GROUPS + turn] for turn in range(GROUPS)]
            heat_flat[pl.ds(offset * HEAT_SLOTS, HEAT_SLOTS), :] = (parts[0] + parts[1]) + (
                parts[2] + parts[3]
            )
        return heat_flat[...]

    def send_heat(kept, own_part, vee, out, target, number):
        mine = dot(take_own, stacked(kept[0]))
        amount = own_part - mine * vee
        flat[pl.ds(0, HEAT_PAD), :] = dot(pool_pick, stacked(amount))
        for offset in range(NEAR):
            out[offset] = flat[pl.ds(offset * HEAT_SLOTS, HEAT_SLOTS), :]
        heat_send(out, target, number)

    def share_copies(buffer, number):
        return group_copies(lambda turn: buffer.at[0], lambda turn: buffer.at[turn], number)

    for copy in vees:
        copy.wait_recv()
    vee = (all_v[0] + all_v[1]) + (all_v[2] + all_v[3])

    far_done(rows_in, recv_sem, ROWS)
    collect_rows(rows_in, share)
    send_heat(share, own_u, vee, heat_out, heat_in, HEAT)
    shares = share_copies(share, SHARE)
    for copy in shares:
        copy.start()
    for copy in gathers:
        copy.wait_recv()
    mix(gathered)
    for copy in shares:
        copy.wait_recv()

    def all_rows(kept):
        return dot(take_turn, stacked(kept[...].reshape(GROUPS * FAR, NZ)))

    cell_temp = all_rows(share)

    def update(channel, total):
        now = cells[channel, pl.ds(1, PX)].reshape(COLS, NZ)
        change = (time_step * drive_gain) * cell_temp * (now - now * now)
        mixing = mixed[channel].reshape(COLS, NZ)
        new = static[channel] - time_step * mixing - change
        shaped = new.reshape(PX, PY, NZ)
        cells2[channel, pl.ds(1, PX)] = shaped
        gathered2[group, channel] = shaped.astype(BF16)
        return total + (new - new * new)

    total = lax.fori_loop(0, CH, update, jnp.zeros((COLS, NZ), F32))
    total = (time_step * drive_gain) * total
    own_v[1] = total
    all_v2[0] = total
    halos2 = halo_copies(cells2, HALO2)
    vees2 = group_copies(lambda turn: own_v.at[1], lambda turn: all_v2.at[turn], VEE2)
    ring2 = ring_copies(gathered2, GATHER2)
    for copy in vees2 + halos2 + ring2[0]:
        copy.start()

    heat_done(heat_in, recv_sem, HEAT)
    arrived = arrived_heat(heat_in)
    spread_rows(warm_rows + heat_gain * dot(relay, stacked(arrived)), rows_out2)
    far_send(rows_out2, rows_in2, ROWS2)
    final_temp[...] = conduct(warm + heat_gain * dot(scatter, stacked(arrived)))

    for copy in halos2:
        copy.wait_recv()
    for arrived_copy, onward in zip(ring2[1], ring2[2]):
        arrived_copy.wait_recv()
        onward.start()
    own_u2 = stencil(cells2, static2)
    for copy in vees2:
        copy.wait_recv()
    vee2 = (all_v2[0] + all_v2[1]) + (all_v2[2] + all_v2[3])

    far_done(rows_in2, recv_sem, ROWS2)
    collect_rows(rows_in2, share2)
    send_heat(share2, own_u2, vee2, heat_out2, heat_in2, HEAT2)
    shares2 = share_copies(share2, SHARE2)
    for copy in shares2:
        copy.start()

    for copy in ring2[3]:
        copy.wait_recv()
    mix(gathered2)
    for copy in shares2:
        copy.wait_recv()
    cell_temp2 = all_rows(share2)

    def finish(channel, _):
        now = cells2[channel, pl.ds(1, PX)].reshape(COLS, NZ)
        change = (time_step * drive_gain) * cell_temp2 * (now - now * now)
        mixing = mixed[channel].reshape(COLS, NZ)
        static2[channel] = static2[channel] - time_step * mixing - change
        return 0

    lax.fori_loop(0, CH, finish, 0)
    store = pltpu.make_async_copy(static2, phases_out, load_sem.at[0])
    store.start()

    heat_done(heat_in2, recv_sem, HEAT2)
    arrived = arrived_heat(heat_in2)
    final_temp[...] = final_temp[...] + heat_gain * dot(scatter, stacked(arrived))
    store_temp = pltpu.make_async_copy(final_temp, temp_out, load_sem.at[1])
    store_temp.start()

    far_done(req_out, send_sem, REQ)
    far_done(rows_out, send_sem, ROWS)
    far_done(rows_out2, send_sem, ROWS2)
    heat_done(heat_in, send_sem, HEAT)
    heat_done(heat_in2, send_sem, HEAT2)
    target_done(target_out, send_sem, TARGET)
    for copy in halos + vees + gathers + shares + halos2 + vees2 + ring2[0] + ring2[2] + shares2:
        copy.wait_send()
    store.wait()
    store_temp.wait()


def place_results(new, temp, new_out, temp_out, new_held, temp_held, load_sem, store_sem):
    moves = [(temp, temp_held, temp_out)] + [
        (new.at[channel], new_held.at[channel], new_out.at[channel]) for channel in range(CH)
    ]
    loads = [
        pltpu.make_async_copy(source, held, load_sem.at[number])
        for number, (source, held, _) in enumerate(moves)
    ]
    stores = [
        pltpu.make_async_copy(held, target, store_sem.at[number])
        for number, (_, held, target) in enumerate(moves)
    ]
    for load in loads:
        load.start()
    for load, store in zip(loads, stores):
        load.wait()
        store.start()
    for store in stores:
        store.wait()


def on_device(
    phases, node_temp, column_nodes, grain_ids, grain_angle, grain_melt, heat_owner, heat_local
):
    outside = pl.BlockSpec(memory_space=pl.ANY)
    vmem, smem = pltpu.VMEM, pltpu.SMEM
    gathered = vmem((GROUPS, CH, PX, PY, NZ), BF16)
    padded = vmem((CH, PX + 2, PY, NZ), F32)
    flat_cells = vmem((CH, COLS, NZ), F32)
    mix_out = vmem((CH, PX, PY, NZ), F32)
    far_rows = vmem((BLOCK, SLOTS, NZ), F32)
    shared = vmem((GROUPS, FAR, NZ), F32)
    heat_out = vmem((NEAR, HEAT_SLOTS, NZ), F32)
    heat_in = vmem((NEAR * GROUPS, HEAT_SLOTS, NZ), F32)
    field = vmem((GROUPS, COLS, NZ), F32)
    new, temp = pl.pallas_call(
        kernel,
        out_shape=(
            jax.ShapeDtypeStruct((CH, COLS, NZ), F32),
            jax.ShapeDtypeStruct(node_temp.shape, F32),
        ),
        in_specs=[outside] * 8,
        out_specs=(outside, outside),
        scratch_shapes=[
            padded, padded, flat_cells, flat_cells, mix_out, gathered, gathered,
            vmem((NODES, NZ), F32), vmem((1, COLS), jnp.int32), smem((SLOT_ALL,), jnp.int32),
            smem((grain_angle.shape[0],), F32), smem((grain_melt.shape[0],), F32),
            smem((POOL,), jnp.int32), smem((POOL,), jnp.int32),
            far_rows, far_rows, far_rows, far_rows, far_rows, far_rows, shared, shared,
            heat_out, heat_in, heat_out, heat_in, heat_out, heat_out,
            vmem((2, COLS, NZ), F32), field, field, vmem((FAR, NZ), F32), vmem((HEAT_PAD, NZ), F32),
            vmem((NODES, NZ), F32),
            pltpu.SemaphoreType.DMA((8,)),
            pltpu.SemaphoreType.DMA((42,)),
            pltpu.SemaphoreType.DMA((42,)),
        ],
        compiler_params=pltpu.CompilerParams(
            collective_id=0, has_side_effects=True, vmem_limit_bytes=56 << 20
        ),
        name="solidify",
    )(
        phases,
        node_temp,
        column_nodes.reshape(1, COLS),
        grain_ids.reshape(SLOT_ALL),
        grain_angle,
        grain_melt,
        heat_owner.reshape(POOL),
        heat_local,
    )
    placed, temp = pl.pallas_call(
        place_results,
        out_shape=(
            jax.ShapeDtypeStruct(new.shape, F32),
            jax.ShapeDtypeStruct(temp.shape, F32),
        ),
        in_specs=[outside] * 2,
        out_specs=(outside, outside),
        scratch_shapes=[
            vmem(new.shape, F32),
            vmem(temp.shape, F32),
            pltpu.SemaphoreType.DMA((CH + 1,)),
            pltpu.SemaphoreType.DMA((CH + 1,)),
        ],
        name="results",
    )(new, temp)
    return placed.reshape(phases.shape), temp


def solution(mesh):
    placed = (
        P("ch", "tile", None, None),
        P("tile", None),
        P("tile"),
        P("tile", None),
        P(),
        P(),
        P("tile", None),
        P("tile"),
    )
    return jax.shard_map(
        on_device,
        mesh=mesh,
        in_specs=placed,
        out_specs=(P("ch", "tile", None, None), P("tile", None)),
        check_vma=False,
    )
```

```python
import functools

import jax
import jax.numpy as jnp
from jax import lax
from jax.experimental import pallas as pl
from jax.experimental.pallas import tpu as pltpu
from jax.sharding import PartitionSpec as P

STEPS = 2
MESH = pl.DeviceIdType.MESH
F32 = jnp.float32
BF16 = jnp.bfloat16

time_step = 0.1
interface_energy = 1.0
drive_gain = 3.0
heat_gain = 0.5
depth_diffusion = 0.2

TILES = 128
GROUPS = 4
BLOCK = TILES // GROUPS
SLOTS = 2
REACH = 3
NEAR = 2 * REACH + 1
HEAT_SLOTS = 4
CH = 8
SLOT_ALL = 32
PX = 8
PY = 16
NZ = 128
COLS = PX * PY
NODES = 256
POOL = 16
FAR = BLOCK * SLOTS
HEAT_ROWS = NEAR * HEAT_SLOTS
HEAT_PAD = 32
QUARTER = CH // 4


def iota(shape, dim):
    return lax.broadcasted_iota(jnp.int32, shape, dim)


def dot(a, b):
    return jnp.dot(a, b, preferred_element_type=F32)


def thirds(value):
    high = value.astype(BF16)
    rest = value - high.astype(F32)
    mid = rest.astype(BF16)
    low = (rest - mid.astype(F32)).astype(BF16)
    return high, mid, low


def stacked(value):
    return jnp.concatenate(thirds(value), axis=0)


def tripled(onehot):
    return jnp.concatenate([onehot, onehot, onehot], axis=1)


def beside(values):
    rows, lanes = values.shape
    lane = iota((rows, lanes), 1)
    up = jnp.where(lane == lanes - 1, 0.0, pltpu.roll(values, lanes - 1, 1))
    down = jnp.where(lane == 0, 0.0, pltpu.roll(values, 1, 1))
    return up + down


def across(values):
    rows, lanes = values.shape
    place = iota((rows, lanes), 0) % PY
    up = jnp.where(place == PY - 1, 0.0, pltpu.roll(values, rows - 1, 0))
    down = jnp.where(place == 0, 0.0, pltpu.roll(values, 1, 0))
    return up + down


def laplacian(padded):
    flat = padded.reshape((PX + 2) * PY, NZ)
    along_y = across(flat)
    inner = (6.0 * along_y - 88.0 * flat) + beside(6.0 * flat + 3.0 * along_y)
    outer = (6.0 * flat + 3.0 * along_y) + beside(3.0 * flat + 2.0 * along_y)
    total = inner[PY:-PY] + (outer[2 * PY :] + outer[: -2 * PY])
    return total * (1.0 / 26.0)


def conduct(rows):
    lane = iota(rows.shape, 1)
    up = jnp.where(lane == NZ - 1, rows, pltpu.roll(rows, NZ - 1, 1))
    down = jnp.where(lane == 0, rows, pltpu.roll(rows, 1, 1))
    return rows + depth_diffusion * (up - 2.0 * rows + down)


def kernel(
    phases_hbm, temp_hbm, columns_hbm, grains_hbm, angle_hbm, melt_hbm, owner_hbm, local_hbm,
    phases_out, temp_out,
    cells, cells2, static, static2, mixed, gathered, gathered2,
    temp, columns, grains, angles, melts, owners, locals_,
    req_out, req_in, rows_out, rows_in, rows_out2, rows_in2, share, share2,
    heat_out, heat_in, heat_out2, heat_in2, target_out, target_in,
    own_v, own_v2, all_v, all_v2, by_owner, flat, heat_flat, final_temp,
    load_sem, send_sem, recv_sem,
):
    tile = lax.axis_index("tile")
    group = lax.axis_index("ch")
    block = tile // BLOCK
    place = tile % BLOCK
    partner = (group + GROUPS - block) % GROUPS
    inside = partner == block

    first = partner * BLOCK
    near_tiles = [lax.rem(tile + (TILES + step - REACH), TILES) for step in range(NEAR)]
    groups = [group] + [lax.rem(group + turn, GROUPS) for turn in range(1, GROUPS)]
    near_order = [
        (offset, turn) for turn in (2, 1, 3, 0) for offset in (0, 6, 1, 5, 2, 4, 3)
    ][:-1]

    def far_index(number):
        half = (number + 1) // 2
        turn = jnp.where(number % 2 == 0, half, BLOCK - half)
        return lax.rem(place + BLOCK // 2 + turn, BLOCK)

    def far_device(index):
        return {"tile": first + index, "ch": group}

    def near_device(offset, turn):
        return {"tile": near_tiles[offset], "ch": groups[turn]}

    barrier = pltpu.get_barrier_semaphore()

    def greet_far(number, _):
        pl.semaphore_signal(
            barrier, inc=1, device_id=far_device(far_index(number)), device_id_type=MESH
        )
        return 0

    lax.fori_loop(0, BLOCK - 1, greet_far, 0)

    @pl.when(jnp.logical_not(inside))
    def _():
        greet_far(BLOCK - 1, 0)

    for offset, turn in near_order:
        pl.semaphore_signal(
            barrier, inc=1, device_id=near_device(offset, turn), device_id_type=MESH
        )

    loads = [
        pltpu.make_async_copy(phases_hbm, cells.at[:, pl.ds(1, PX)], load_sem.at[0]),
        pltpu.make_async_copy(temp_hbm, temp, load_sem.at[1]),
        pltpu.make_async_copy(columns_hbm, columns, load_sem.at[2]),
        pltpu.make_async_copy(grains_hbm, grains, load_sem.at[3]),
        pltpu.make_async_copy(angle_hbm, angles, load_sem.at[4]),
        pltpu.make_async_copy(melt_hbm, melts, load_sem.at[5]),
        pltpu.make_async_copy(owner_hbm, owners, load_sem.at[6]),
        pltpu.make_async_copy(local_hbm, locals_, load_sem.at[7]),
    ]
    for load in loads:
        load.start()
    for load in loads:
        load.wait()

    wanted = jnp.broadcast_to(columns[...].astype(F32), (COLS, COLS))
    wanted_down = wanted.T
    wanted_i = wanted.astype(jnp.int32)
    wanted_down_i = wanted_down.astype(jnp.int32)
    owner_over = wanted_i // NODES
    owner_down = wanted_down_i // NODES
    local_down = (wanted_down_i % NODES).astype(F32)
    down, over = iota((COLS, COLS), 0), iota((COLS, COLS), 1)
    same = owner_over == owner_down
    slot_over = jnp.sum(jnp.where(same & (down < over), 1.0, 0.0), axis=0, keepdims=True)
    slot_down = jnp.sum(jnp.where(same & (over < down), 1.0, 0.0), axis=1, keepdims=True)
    key_over = owner_over[:1] * SLOTS + slot_over.astype(jnp.int32)
    key_down = owner_down[:, :1] * SLOTS + slot_down.astype(jnp.int32)
    ask = jnp.where(iota((FAR, COLS), 0) + partner * FAR == key_over, 1.0, 0.0).astype(BF16)
    flat[pl.ds(0, FAR), :] = dot(ask, local_down.astype(BF16))
    for index in range(BLOCK):
        req_out[index] = flat[pl.ds(index * SLOTS, SLOTS), :]
    key_lane = iota((COLS, FAR), 1)
    take_own = jnp.where(key_lane + partner * FAR == key_down, 1.0, 0.0).astype(BF16)
    row_all = iota((GROUPS * FAR, COLS), 0)
    row_block = ((group + row_all // FAR) % GROUPS + GROUPS - block) % GROUPS
    give_all = jnp.where(row_block * FAR + row_all % FAR == key_over, 1.0, 0.0).astype(BF16)
    give_all = tripled(give_all)
    lane_all = iota((COLS, GROUPS * FAR), 1)
    lane_group = (group + GROUPS - lane_all // FAR) % GROUPS
    lane_block = (lane_group + GROUPS - block) % GROUPS
    take_turn = jnp.where(
        lane_block * FAR + lane_all % FAR == key_down, 1.0, 0.0
    ).astype(BF16)
    take_turn = tripled(take_turn)

    row_down, lane = iota((POOL, COLS), 0), iota((POOL, COLS), 1)
    off_down = jnp.zeros((POOL, COLS), jnp.int32)
    off_over = jnp.zeros((POOL, COLS), jnp.int32)
    local_rows = jnp.zeros((POOL, NZ), jnp.int32)
    for row in range(POOL):
        off = (owners[row] - tile + (REACH + TILES)) % TILES
        off_down = jnp.where(row_down == row, off, off_down)
        off_over = jnp.where(lane // 8 == row, off, off_over)
        local_rows = jnp.where(row_down == row, locals_[row], local_rows)
    earlier = jnp.where((off_down == off_over) & (row_down < lane // 8), 1.0, 0.0)
    heat_slot = jnp.sum(earlier, axis=0, keepdims=True).astype(jnp.int32)
    heat_key = off_over[:1] * HEAT_SLOTS + heat_slot
    spread = iota((HEAT_PAD, COLS), 0) == heat_key
    pool_pick = jnp.where(spread, 1.0, 0.0).astype(BF16)
    row_of = jnp.where(iota((COLS, POOL), 0) == 8 * iota((COLS, POOL), 1), 1.0, 0.0).astype(BF16)
    row_pick = dot(pool_pick, row_of).astype(BF16)
    slot_pick = tripled(dot(pool_pick, take_own).astype(BF16))
    pool_pick = tripled(pool_pick)
    flat[pl.ds(0, HEAT_PAD), :] = dot(row_pick, local_rows.astype(F32).astype(BF16))
    for offset in range(NEAR):
        target_out[offset] = flat[pl.ds(offset * HEAT_SLOTS, HEAT_SLOTS), :]

    def first_look(channel, total):
        now = cells[channel, pl.ds(1, PX)]
        gathered[group, channel] = now.astype(BF16)
        return total + (now - now * now)

    total = lax.fori_loop(0, CH, first_look, jnp.zeros((PX, PY, NZ), F32))
    total = (time_step * drive_gain) * total.reshape(COLS, NZ)
    own_v[...] = dot(give_all, stacked(total)).reshape(GROUPS, FAR, NZ)

    warm = conduct(temp[...])
    cold_parts, warm_parts = stacked(temp[...]), stacked(warm)

    pl.semaphore_wait(
        barrier, NEAR * GROUPS - 1 + jnp.where(inside, BLOCK - 1, BLOCK).astype(jnp.int32)
    )

    def far_copy(source, target, index, number):
        return pltpu.make_async_remote_copy(
            src_ref=source.at[index],
            dst_ref=target.at[place],
            send_sem=send_sem.at[number],
            recv_sem=recv_sem.at[number],
            device_id=far_device(index),
            device_id_type=MESH,
        )

    def far_send(source, target, number):
        def one(order, _):
            far_copy(source, target, far_index(order), number).start()
            return 0

        lax.fori_loop(0, BLOCK - 1, one, 0)

        @pl.when(jnp.logical_not(inside))
        def _():
            one(BLOCK - 1, 0)

        @pl.when(inside)
        def _():
            target[place] = source[place]

    def far_done(buffer, sem, number):
        @pl.when(inside)
        def _():
            part = buffer.at[pl.ds(0, BLOCK - 1)]
            pltpu.make_async_copy(part, part, sem.at[number]).wait()

        @pl.when(jnp.logical_not(inside))
        def _():
            pltpu.make_async_copy(buffer, buffer, sem.at[number]).wait()

    def heat_send(source, target, number):
        for offset, turn in near_order:
            pltpu.make_async_remote_copy(
                src_ref=source.at[offset],
                dst_ref=target.at[offset * GROUPS + group],
                send_sem=send_sem.at[number],
                recv_sem=recv_sem.at[number],
                device_id=near_device(offset, turn),
                device_id_type=MESH,
            ).start()
        target[REACH * GROUPS + group] = source[REACH]

    def heat_done(buffer, sem, number):
        part = buffer.at[pl.ds(0, NEAR * GROUPS - 1)]
        pltpu.make_async_copy(part, part, sem.at[number]).wait()

    def target_send(number):
        for offset in (0, 6, 1, 5, 2, 4):
            pltpu.make_async_remote_copy(
                src_ref=target_out.at[offset],
                dst_ref=target_in.at[offset],
                send_sem=send_sem.at[number],
                recv_sem=recv_sem.at[number],
                device_id=near_device(offset, 0),
                device_id_type=MESH,
            ).start()
        target_in[REACH] = target_out[REACH]

    def target_done(buffer, sem, number):
        part = buffer.at[pl.ds(0, NEAR - 1)]
        pltpu.make_async_copy(part, part, sem.at[number]).wait()

    def group_copies(source_of, target_of, number):
        return [
            pltpu.make_async_remote_copy(
                src_ref=source_of(turn),
                dst_ref=target_of(turn),
                send_sem=send_sem.at[number + turn],
                recv_sem=recv_sem.at[number + turn],
                device_id=near_device(REACH, turn),
                device_id_type=MESH,
            )
            for turn in range(1, GROUPS)
        ]

    def ring_copies(buffer, number):
        def move(owner, part, turn, order):
            piece = buffer.at[owner, pl.ds(part * QUARTER, QUARTER)]
            return pltpu.make_async_remote_copy(
                src_ref=piece,
                dst_ref=piece,
                send_sem=send_sem.at[number + order],
                recv_sem=recv_sem.at[number + order],
                device_id=near_device(REACH, turn),
                device_id_type=MESH,
            )

        right = [move(group, part, 1, part) for part in (0, 1, 2, 3)]
        left = [move(group, part, 3, 4 + part) for part in (2, 3, 0, 1)]
        starts = [copy for pair in zip(right, left) for copy in pair]
        onward = []
        for step in range(2):
            onward.append(move(groups[3], step, 1, 8 + step))
            onward.append(move(groups[1], step + 2, 3, 10 + step))
        return starts, starts[:4], onward, starts[4:] + onward

    def halo_copies(buffer, number):
        return [
            pltpu.make_async_remote_copy(
                src_ref=buffer.at[:, 1],
                dst_ref=buffer.at[:, PX + 1],
                send_sem=send_sem.at[number],
                recv_sem=recv_sem.at[number],
                device_id=near_device(REACH - 1, 0),
                device_id_type=MESH,
            ),
            pltpu.make_async_remote_copy(
                src_ref=buffer.at[:, PX],
                dst_ref=buffer.at[:, 0],
                send_sem=send_sem.at[number + 1],
                recv_sem=recv_sem.at[number + 1],
                device_id=near_device(REACH + 1, 0),
                device_id_type=MESH,
            ),
        ]

    REQ, ROWS, ROWS2, HEAT, HEAT2, TARGET = 0, 1, 2, 3, 4, 5
    HALO, HALO2 = 6, 8
    GATHER, GATHER2, SHARE, SHARE2, VEE, VEE2 = 10, 14, 26, 30, 34, 38

    far_send(req_out, req_in, REQ)
    target_send(TARGET)
    halos = halo_copies(cells, HALO)
    vees = group_copies(lambda turn: own_v.at[turn], lambda turn: all_v.at[turn], VEE)
    gathers = group_copies(
        lambda turn: gathered.at[group], lambda turn: gathered.at[group], GATHER
    )
    for copy in halos + vees + gathers:
        copy.start()

    angle_down = jnp.zeros((SLOT_ALL, NZ), F32)
    angle_over = jnp.zeros((SLOT_ALL, NZ), F32)
    slot_row, slot_lane = iota((SLOT_ALL, NZ), 0), iota((SLOT_ALL, NZ), 1)
    for slot in range(SLOT_ALL):
        angle = angles[grains[slot]]
        angle_down = jnp.where(slot_row == slot, angle, angle_down)
        angle_over = jnp.where(slot_lane == slot, angle, angle_over)
    strength = interface_energy / SLOT_ALL * (0.3 + jnp.abs(jnp.sin(angle_down - angle_over)))
    strength = jnp.where((slot_row != slot_lane) & (slot_lane < SLOT_ALL), strength, 0.0)
    strength = strength.astype(BF16)
    column_sums = jnp.sum(strength.astype(F32), axis=0, keepdims=True)
    own_row = iota((COLS, SLOT_ALL), 0) // PY + group * CH
    choose = jnp.where(own_row == iota((COLS, SLOT_ALL), 1), 1.0, 0.0).astype(BF16)
    tall = dot(choose, strength).astype(BF16)
    wide_shape = (NZ, SLOT_ALL * PY)
    widen = jnp.where(iota(wide_shape, 0) == iota(wide_shape, 1) // PY, 1.0, 0.0).astype(BF16)
    weights = dot(tall, widen)
    weights = jnp.where(iota(wide_shape, 0) % PY == iota(wide_shape, 1) % PY, weights, 0.0)
    weights = weights.astype(BF16)
    for owner in range(GROUPS):
        by_owner[owner] = weights[:, owner * COLS : (owner + 1) * COLS]

    def melt_of(channel):
        return melts[grains[group * CH + channel]]

    def sum_of(channel):
        lanes = iota((1, NZ), 1) == group * CH + channel
        return jnp.sum(jnp.where(lanes, column_sums, 0.0), axis=1, keepdims=True)

    def stencil(buffer, kept):
        @pl.when(tile == 0)
        def _():
            buffer[:, 0] = jnp.zeros((CH, PY, NZ), F32)

        @pl.when(tile == TILES - 1)
        def _():
            buffer[:, PX + 1] = jnp.zeros((CH, PY, NZ), F32)

        def one(channel, total):
            padded = buffer[channel]
            now = padded[1:-1].reshape(COLS, NZ)
            gain = time_step * laplacian(padded)
            gain = gain + (melt_of(channel) * (time_step * drive_gain)) * (now - now * now)
            kept[channel] = now + gain
            rounded = now.astype(BF16).astype(F32)
            return total + (gain - (time_step * sum_of(channel)) * rounded)

        return lax.fori_loop(0, CH, one, jnp.zeros((COLS, NZ), F32))

    def mix(buffer):
        for plane in range(PX):
            right = buffer[:, :, plane].reshape(SLOT_ALL * PY, NZ)
            mixed[:, plane] = dot(weights, right).reshape(CH, PY, NZ)

    for copy in halos:
        copy.wait_recv()
    own_u = stencil(cells, static)

    far_done(req_in, recv_sem, REQ)
    for index in range(BLOCK):
        flat[pl.ds(index * SLOTS, SLOTS), :] = req_in[index]
    asked = flat[pl.ds(0, FAR), :].astype(jnp.int32)
    asked = jnp.concatenate([asked, asked], axis=1)
    serve = jnp.where(asked == iota((FAR, NODES), 1), 1.0, 0.0).astype(BF16)

    def spread_rows(values, out):
        flat[pl.ds(0, FAR), :] = values
        for index in range(BLOCK):
            out[index] = flat[pl.ds(index * SLOTS, SLOTS), :]

    def collect_rows(buffer, kept):
        for index in range(BLOCK):
            kept[0, pl.ds(index * SLOTS, SLOTS), :] = buffer[index]

    serve = tripled(serve)
    spread_rows(dot(serve, cold_parts), rows_out)
    far_send(rows_out, rows_in, ROWS)

    target_done(target_in, recv_sem, TARGET)
    heat_flat[...] = jnp.full((HEAT_PAD, NZ), -1.0, F32)
    for offset in range(NEAR):
        heat_flat[pl.ds(offset * HEAT_SLOTS, HEAT_SLOTS), :] = target_in[offset]
    aims = heat_flat[...].astype(jnp.int32)
    aims = jnp.concatenate([aims, jnp.full((NZ - HEAT_PAD, NZ), -1, jnp.int32)], axis=0)
    low = jnp.where(aims == iota((NZ, NZ), 1), 1.0, 0.0).T
    high = jnp.where(aims == iota((NZ, NZ), 1) + NZ, 1.0, 0.0).T
    scatter = jnp.concatenate([low, high], axis=0)[:, :HEAT_PAD].astype(BF16)
    relay = tripled(dot(serve[:, :NODES], scatter).astype(BF16))
    scatter = tripled(scatter)
    warm_rows = dot(serve, warm_parts)
    heat_flat[...] = jnp.zeros((HEAT_PAD, NZ), F32)

    def arrived_heat(buffer):
        for offset in range(NEAR):
            parts = [buffer[offset * GROUPS + turn] for turn in range(GROUPS)]
            heat_flat[pl.ds(offset * HEAT_SLOTS, HEAT_SLOTS), :] = (parts[0] + parts[1]) + (
                parts[2] + parts[3]
            )
        return heat_flat[...]

    def send_heat(kept, own_part, vee, out, target, number):
        warmed = dot(slot_pick, stacked(kept[0] * vee))
        flat[pl.ds(0, HEAT_PAD), :] = own_part - warmed
        for offset in range(NEAR):
            out[offset] = flat[pl.ds(offset * HEAT_SLOTS, HEAT_SLOTS), :]
        heat_send(out, target, number)

    def share_copies(buffer, number):
        return group_copies(lambda turn: buffer.at[0], lambda turn: buffer.at[turn], number)

    for copy in vees:
        copy.wait_recv()
    vee = (own_v[0] + all_v[1]) + (all_v[2] + all_v[3])
    fixed_heat = dot(pool_pick, stacked(own_u))

    far_done(rows_in, recv_sem, ROWS)
    collect_rows(rows_in, share)
    send_heat(share, fixed_heat, vee, heat_out, heat_in, HEAT)
    shares = share_copies(share, SHARE)
    for copy in shares:
        copy.start()
    for copy in gathers:
        copy.wait_recv()
    mix(gathered)
    for copy in shares:
        copy.wait_recv()

    def all_rows(kept):
        return dot(take_turn, stacked(kept[...].reshape(GROUPS * FAR, NZ)))

    cell_temp = all_rows(share)

    def update(channel, total):
        now = cells[channel, pl.ds(1, PX)].reshape(COLS, NZ)
        change = (time_step * drive_gain) * cell_temp * (now - now * now)
        mixing = mixed[channel].reshape(COLS, NZ)
        new = static[channel] - time_step * mixing - change
        shaped = new.reshape(PX, PY, NZ)
        cells2[channel, pl.ds(1, PX)] = shaped
        gathered2[group, channel] = shaped.astype(BF16)
        return total + (new - new * new)

    total = lax.fori_loop(0, CH, update, jnp.zeros((COLS, NZ), F32))
    total = (time_step * drive_gain) * total
    own_v2[...] = dot(give_all, stacked(total)).reshape(GROUPS, FAR, NZ)
    halos2 = halo_copies(cells2, HALO2)
    vees2 = group_copies(lambda turn: own_v2.at[turn], lambda turn: all_v2.at[turn], VEE2)
    ring2 = ring_copies(gathered2, GATHER2)
    for copy in vees2 + halos2 + ring2[0]:
        copy.start()

    heat_done(heat_in, recv_sem, HEAT)
    arrived = arrived_heat(heat_in)
    spread_rows(warm_rows + heat_gain * dot(relay, stacked(arrived)), rows_out2)
    far_send(rows_out2, rows_in2, ROWS2)
    final_temp[...] = conduct(warm + heat_gain * dot(scatter, stacked(arrived)))

    for copy in halos2:
        copy.wait_recv()
    for arrived_copy, onward in zip(ring2[1], ring2[2]):
        arrived_copy.wait_recv()
        onward.start()
    own_u2 = stencil(cells2, static2)
    for copy in vees2:
        copy.wait_recv()
    vee2 = (own_v2[0] + all_v2[1]) + (all_v2[2] + all_v2[3])
    fixed_heat2 = dot(pool_pick, stacked(own_u2))

    far_done(rows_in2, recv_sem, ROWS2)
    collect_rows(rows_in2, share2)
    send_heat(share2, fixed_heat2, vee2, heat_out2, heat_in2, HEAT2)
    shares2 = share_copies(share2, SHARE2)
    for copy in shares2:
        copy.start()

    for copy in ring2[3][:4]:
        copy.wait_recv()

    def block_of(owner, plane):
        right = gathered2[owner, :, plane].reshape(COLS, NZ)
        return dot(by_owner[owner], right).reshape(CH, PY, NZ)

    for plane in range(PX):
        mixed[:, plane] = block_of(group, plane) + (
            block_of(groups[1], plane) + block_of(groups[3], plane)
        )
    for copy in ring2[3][4:]:
        copy.wait_recv()
    for plane in range(PX):
        mixed[:, plane] += block_of(groups[2], plane)
    for copy in shares2:
        copy.wait_recv()
    cell_temp2 = all_rows(share2)

    def finish(channel, _):
        now = cells2[channel, pl.ds(1, PX)].reshape(COLS, NZ)
        change = (time_step * drive_gain) * cell_temp2 * (now - now * now)
        mixing = mixed[channel].reshape(COLS, NZ)
        static2[channel] = static2[channel] - time_step * mixing - change
        return 0

    lax.fori_loop(0, CH, finish, 0)
    store = pltpu.make_async_copy(static2, phases_out, load_sem.at[0])
    store.start()

    heat_done(heat_in2, recv_sem, HEAT2)
    arrived = arrived_heat(heat_in2)
    final_temp[...] = final_temp[...] + heat_gain * dot(scatter, stacked(arrived))
    store_temp = pltpu.make_async_copy(final_temp, temp_out, load_sem.at[1])
    store_temp.start()

    far_done(req_out, send_sem, REQ)
    far_done(rows_out, send_sem, ROWS)
    far_done(rows_out2, send_sem, ROWS2)
    heat_done(heat_in, send_sem, HEAT)
    heat_done(heat_in2, send_sem, HEAT2)
    target_done(target_out, send_sem, TARGET)
    for copy in halos + vees + gathers + shares + halos2 + vees2 + ring2[0] + ring2[2] + shares2:
        copy.wait_send()
    store.wait()
    store_temp.wait()


def place_results(new, temp, new_out, temp_out, new_held, temp_held, load_sem, store_sem):
    moves = [(temp, temp_held, temp_out)] + [
        (new.at[channel], new_held.at[channel], new_out.at[channel]) for channel in range(CH)
    ]
    loads = [
        pltpu.make_async_copy(source, held, load_sem.at[number])
        for number, (source, held, _) in enumerate(moves)
    ]
    stores = [
        pltpu.make_async_copy(held, target, store_sem.at[number])
        for number, (_, held, target) in enumerate(moves)
    ]
    for load in loads:
        load.start()
    for load, store in zip(loads, stores):
        load.wait()
        store.start()
    for store in stores:
        store.wait()


def on_device(
    phases, node_temp, column_nodes, grain_ids, grain_angle, grain_melt, heat_owner, heat_local
):
    outside = pl.BlockSpec(memory_space=pl.ANY)
    vmem, smem = pltpu.VMEM, pltpu.SMEM
    gathered = vmem((GROUPS, CH, PX, PY, NZ), BF16)
    padded = vmem((CH, PX + 2, PY, NZ), F32)
    flat_cells = vmem((CH, COLS, NZ), F32)
    mix_out = vmem((CH, PX, PY, NZ), F32)
    far_rows = vmem((BLOCK, SLOTS, NZ), F32)
    shared = vmem((GROUPS, FAR, NZ), F32)
    heat_out = vmem((NEAR, HEAT_SLOTS, NZ), F32)
    heat_in = vmem((NEAR * GROUPS, HEAT_SLOTS, NZ), F32)
    new, temp = pl.pallas_call(
        kernel,
        out_shape=(
            jax.ShapeDtypeStruct((CH, COLS, NZ), F32),
            jax.ShapeDtypeStruct(node_temp.shape, F32),
        ),
        in_specs=[outside] * 8,
        out_specs=(outside, outside),
        scratch_shapes=[
            padded, padded, flat_cells, flat_cells, mix_out, gathered, gathered,
            vmem((NODES, NZ), F32), vmem((1, COLS), jnp.int32), smem((SLOT_ALL,), jnp.int32),
            smem((grain_angle.shape[0],), F32), smem((grain_melt.shape[0],), F32),
            smem((POOL,), jnp.int32), smem((POOL,), jnp.int32),
            far_rows, far_rows, far_rows, far_rows, far_rows, far_rows, shared, shared,
            heat_out, heat_in, heat_out, heat_in, heat_out, heat_out,
            shared, shared, shared, shared, vmem((GROUPS, COLS, COLS), BF16), vmem((FAR, NZ), F32), vmem((HEAT_PAD, NZ), F32),
            vmem((NODES, NZ), F32),
            pltpu.SemaphoreType.DMA((8,)),
            pltpu.SemaphoreType.DMA((42,)),
            pltpu.SemaphoreType.DMA((42,)),
        ],
        compiler_params=pltpu.CompilerParams(
            collective_id=0, has_side_effects=True, vmem_limit_bytes=56 << 20
        ),
        name="solidify",
    )(
        phases,
        node_temp,
        column_nodes.reshape(1, COLS),
        grain_ids.reshape(SLOT_ALL),
        grain_angle,
        grain_melt,
        heat_owner.reshape(POOL),
        heat_local,
    )
    placed, temp = pl.pallas_call(
        place_results,
        out_shape=(
            jax.ShapeDtypeStruct(new.shape, F32),
            jax.ShapeDtypeStruct(temp.shape, F32),
        ),
        in_specs=[outside] * 2,
        out_specs=(outside, outside),
        scratch_shapes=[
            vmem(new.shape, F32),
            vmem(temp.shape, F32),
            pltpu.SemaphoreType.DMA((CH + 1,)),
            pltpu.SemaphoreType.DMA((CH + 1,)),
        ],
        name="results",
    )(new, temp)
    return placed.reshape(phases.shape), temp


def solution(mesh):
    placed = (
        P("ch", "tile", None, None),
        P("tile", None),
        P("tile"),
        P("tile", None),
        P(),
        P(),
        P("tile", None),
        P("tile"),
    )
    return jax.shard_map(
        on_device,
        mesh=mesh,
        in_specs=placed,
        out_specs=(P("ch", "tile", None, None), P("tile", None)),
        check_vma=False,
    )
```

```python
import functools

import jax
import jax.numpy as jnp
from jax import lax
from jax.experimental import pallas as pl
from jax.experimental.pallas import tpu as pltpu
from jax.sharding import PartitionSpec as P

STEPS = 2
MESH = pl.DeviceIdType.MESH
F32 = jnp.float32
BF16 = jnp.bfloat16

time_step = 0.1
interface_energy = 1.0
drive_gain = 3.0
heat_gain = 0.5
depth_diffusion = 0.2

TILES = 128
GROUPS = 4
BLOCK = TILES // GROUPS
SLOTS = 2
REACH = 3
NEAR = 2 * REACH + 1
HEAT_SLOTS = 4
CH = 8
SLOT_ALL = 32
PX = 8
PY = 16
NZ = 128
COLS = PX * PY
NODES = 256
POOL = 16
FAR = BLOCK * SLOTS
HEAT_ROWS = NEAR * HEAT_SLOTS
HEAT_PAD = 32
QUARTER = CH // 4


def iota(shape, dim):
    return lax.broadcasted_iota(jnp.int32, shape, dim)


def dot(a, b):
    return jnp.dot(a, b, preferred_element_type=F32)


def thirds(value):
    high = value.astype(BF16)
    rest = value - high.astype(F32)
    mid = rest.astype(BF16)
    low = (rest - mid.astype(F32)).astype(BF16)
    return high, mid, low


def stacked(value):
    return jnp.concatenate(thirds(value), axis=0)


def tripled(onehot):
    return jnp.concatenate([onehot, onehot, onehot], axis=1)


def beside(values):
    rows, lanes = values.shape
    lane = iota((rows, lanes), 1)
    up = jnp.where(lane == lanes - 1, 0.0, pltpu.roll(values, lanes - 1, 1))
    down = jnp.where(lane == 0, 0.0, pltpu.roll(values, 1, 1))
    return up + down


def across(values):
    rows, lanes = values.shape
    place = iota((rows, lanes), 0) % PY
    up = jnp.where(place == PY - 1, 0.0, pltpu.roll(values, rows - 1, 0))
    down = jnp.where(place == 0, 0.0, pltpu.roll(values, 1, 0))
    return up + down


def laplacian(padded):
    flat = padded.reshape((PX + 2) * PY, NZ)
    along_y = across(flat)
    inner = (6.0 * along_y - 88.0 * flat) + beside(6.0 * flat + 3.0 * along_y)
    outer = (6.0 * flat + 3.0 * along_y) + beside(3.0 * flat + 2.0 * along_y)
    total = inner[PY:-PY] + (outer[2 * PY :] + outer[: -2 * PY])
    return total * (1.0 / 26.0)


def conduct(rows):
    lane = iota(rows.shape, 1)
    up = jnp.where(lane == NZ - 1, rows, pltpu.roll(rows, NZ - 1, 1))
    down = jnp.where(lane == 0, rows, pltpu.roll(rows, 1, 1))
    return rows + depth_diffusion * (up - 2.0 * rows + down)


def kernel(
    phases_hbm, temp_hbm, columns_hbm, grains_hbm, angle_hbm, melt_hbm, owner_hbm, local_hbm,
    phases_out, temp_out,
    cells, cells2, static, static2, mixed, gathered, gathered2,
    temp, columns, grains, angles, melts, owners, locals_,
    req_out, req_in, rows_out, rows_in, rows_out2, rows_in2, share, share2,
    heat_out, heat_in, heat_out2, heat_in2, target_out, target_in,
    own_v, own_v2, all_v, all_v2, by_owner, flat, heat_flat, final_temp,
    load_sem, send_sem, recv_sem,
):
    tile = lax.axis_index("tile")
    group = lax.axis_index("ch")
    block = tile // BLOCK
    place = tile % BLOCK
    partner = (group + GROUPS - block) % GROUPS
    inside = partner == block

    first = partner * BLOCK
    near_tiles = [lax.rem(tile + (TILES + step - REACH), TILES) for step in range(NEAR)]
    groups = [group] + [lax.rem(group + turn, GROUPS) for turn in range(1, GROUPS)]
    near_order = [
        (offset, turn) for turn in (2, 1, 3, 0) for offset in (0, 6, 1, 5, 2, 4, 3)
    ][:-1]

    def far_index(number):
        half = (number + 1) // 2
        turn = jnp.where(number % 2 == 0, half, BLOCK - half)
        return lax.rem(place + BLOCK // 2 + turn, BLOCK)

    def far_device(index):
        return {"tile": first + index, "ch": group}

    def near_device(offset, turn):
        return {"tile": near_tiles[offset], "ch": groups[turn]}

    barrier = pltpu.get_barrier_semaphore()

    def greet_far(number, _):
        pl.semaphore_signal(
            barrier, inc=1, device_id=far_device(far_index(number)), device_id_type=MESH
        )
        return 0

    lax.fori_loop(0, BLOCK - 1, greet_far, 0)

    @pl.when(jnp.logical_not(inside))
    def _():
        greet_far(BLOCK - 1, 0)

    for offset, turn in near_order:
        pl.semaphore_signal(
            barrier, inc=1, device_id=near_device(offset, turn), device_id_type=MESH
        )

    loads = [
        pltpu.make_async_copy(phases_hbm, cells.at[:, pl.ds(1, PX)], load_sem.at[0]),
        pltpu.make_async_copy(temp_hbm, temp, load_sem.at[1]),
        pltpu.make_async_copy(columns_hbm, columns, load_sem.at[2]),
        pltpu.make_async_copy(grains_hbm, grains, load_sem.at[3]),
        pltpu.make_async_copy(angle_hbm, angles, load_sem.at[4]),
        pltpu.make_async_copy(melt_hbm, melts, load_sem.at[5]),
        pltpu.make_async_copy(owner_hbm, owners, load_sem.at[6]),
        pltpu.make_async_copy(local_hbm, locals_, load_sem.at[7]),
    ]
    for load in loads:
        load.start()
    for load in loads:
        load.wait()

    wanted = jnp.broadcast_to(columns[...].astype(F32), (COLS, COLS))
    wanted_down = wanted.T
    wanted_i = wanted.astype(jnp.int32)
    wanted_down_i = wanted_down.astype(jnp.int32)
    owner_over = wanted_i // NODES
    owner_down = wanted_down_i // NODES
    local_down = (wanted_down_i % NODES).astype(F32)
    down, over = iota((COLS, COLS), 0), iota((COLS, COLS), 1)
    same = owner_over == owner_down
    slot_over = jnp.sum(jnp.where(same & (down < over), 1.0, 0.0), axis=0, keepdims=True)
    slot_down = jnp.sum(jnp.where(same & (over < down), 1.0, 0.0), axis=1, keepdims=True)
    key_over = owner_over[:1] * SLOTS + slot_over.astype(jnp.int32)
    key_down = owner_down[:, :1] * SLOTS + slot_down.astype(jnp.int32)
    ask = jnp.where(iota((FAR, COLS), 0) + partner * FAR == key_over, 1.0, 0.0).astype(BF16)
    flat[pl.ds(0, FAR), :] = dot(ask, local_down.astype(BF16))
    for index in range(BLOCK):
        req_out[index] = flat[pl.ds(index * SLOTS, SLOTS), :]
    key_lane = iota((COLS, FAR), 1)
    take_own = jnp.where(key_lane + partner * FAR == key_down, 1.0, 0.0).astype(BF16)
    row_all = iota((GROUPS * FAR, COLS), 0)
    row_block = ((group + row_all // FAR) % GROUPS + GROUPS - block) % GROUPS
    give_all = jnp.where(row_block * FAR + row_all % FAR == key_over, 1.0, 0.0).astype(BF16)
    give_all = tripled(give_all)
    lane_all = iota((COLS, GROUPS * FAR), 1)
    lane_group = (group + GROUPS - lane_all // FAR) % GROUPS
    lane_block = (lane_group + GROUPS - block) % GROUPS
    take_turn = jnp.where(
        lane_block * FAR + lane_all % FAR == key_down, 1.0, 0.0
    ).astype(BF16)
    take_turn = tripled(take_turn)

    row_down, lane = iota((POOL, COLS), 0), iota((POOL, COLS), 1)
    off_down = jnp.zeros((POOL, COLS), jnp.int32)
    off_over = jnp.zeros((POOL, COLS), jnp.int32)
    local_rows = jnp.zeros((POOL, NZ), jnp.int32)
    for row in range(POOL):
        off = (owners[row] - tile + (REACH + TILES)) % TILES
        off_down = jnp.where(row_down == row, off, off_down)
        off_over = jnp.where(lane // 8 == row, off, off_over)
        local_rows = jnp.where(row_down == row, locals_[row], local_rows)
    earlier = jnp.where((off_down == off_over) & (row_down < lane // 8), 1.0, 0.0)
    heat_slot = jnp.sum(earlier, axis=0, keepdims=True).astype(jnp.int32)
    heat_key = off_over[:1] * HEAT_SLOTS + heat_slot
    spread = iota((HEAT_PAD, COLS), 0) == heat_key
    pool_pick = jnp.where(spread, 1.0, 0.0).astype(BF16)
    row_of = jnp.where(iota((COLS, POOL), 0) == 8 * iota((COLS, POOL), 1), 1.0, 0.0).astype(BF16)
    row_pick = dot(pool_pick, row_of).astype(BF16)
    slot_pick = tripled(dot(pool_pick, take_own).astype(BF16))
    pool_pick = tripled(pool_pick)
    flat[pl.ds(0, HEAT_PAD), :] = dot(row_pick, local_rows.astype(F32).astype(BF16))
    for offset in range(NEAR):
        target_out[offset] = flat[pl.ds(offset * HEAT_SLOTS, HEAT_SLOTS), :]

    def first_look(channel, total):
        now = cells[channel, pl.ds(1, PX)]
        gathered[group, channel] = now.astype(BF16)
        return total + (now - now * now)

    total = lax.fori_loop(0, CH, first_look, jnp.zeros((PX, PY, NZ), F32))
    total = (time_step * drive_gain) * total.reshape(COLS, NZ)
    own_v[...] = dot(give_all, stacked(total)).reshape(GROUPS, FAR, NZ)

    warm = conduct(temp[...])
    cold_parts, warm_parts = stacked(temp[...]), stacked(warm)

    pl.semaphore_wait(
        barrier, NEAR * GROUPS - 1 + jnp.where(inside, BLOCK - 1, BLOCK).astype(jnp.int32)
    )

    def far_copy(source, target, index, number):
        return pltpu.make_async_remote_copy(
            src_ref=source.at[index],
            dst_ref=target.at[place],
            send_sem=send_sem.at[number],
            recv_sem=recv_sem.at[number],
            device_id=far_device(index),
            device_id_type=MESH,
        )

    def far_send(source, target, number):
        def one(order, _):
            far_copy(source, target, far_index(order), number).start()
            return 0

        lax.fori_loop(0, BLOCK - 1, one, 0)

        @pl.when(jnp.logical_not(inside))
        def _():
            one(BLOCK - 1, 0)

        @pl.when(inside)
        def _():
            target[place] = source[place]

    def far_done(buffer, sem, number):
        @pl.when(inside)
        def _():
            part = buffer.at[pl.ds(0, BLOCK - 1)]
            pltpu.make_async_copy(part, part, sem.at[number]).wait()

        @pl.when(jnp.logical_not(inside))
        def _():
            pltpu.make_async_copy(buffer, buffer, sem.at[number]).wait()

    def heat_send(source, target, number):
        for offset, turn in near_order:
            pltpu.make_async_remote_copy(
                src_ref=source.at[offset],
                dst_ref=target.at[offset * GROUPS + group],
                send_sem=send_sem.at[number],
                recv_sem=recv_sem.at[number],
                device_id=near_device(offset, turn),
                device_id_type=MESH,
            ).start()
        target[REACH * GROUPS + group] = source[REACH]

    def heat_done(buffer, sem, number):
        part = buffer.at[pl.ds(0, NEAR * GROUPS - 1)]
        pltpu.make_async_copy(part, part, sem.at[number]).wait()

    def target_send(number):
        for offset in (0, 6, 1, 5, 2, 4):
            pltpu.make_async_remote_copy(
                src_ref=target_out.at[offset],
                dst_ref=target_in.at[offset],
                send_sem=send_sem.at[number],
                recv_sem=recv_sem.at[number],
                device_id=near_device(offset, 0),
                device_id_type=MESH,
            ).start()
        target_in[REACH] = target_out[REACH]

    def target_done(buffer, sem, number):
        part = buffer.at[pl.ds(0, NEAR - 1)]
        pltpu.make_async_copy(part, part, sem.at[number]).wait()

    def group_copies(source_of, target_of, number):
        return [
            pltpu.make_async_remote_copy(
                src_ref=source_of(turn),
                dst_ref=target_of(turn),
                send_sem=send_sem.at[number + turn],
                recv_sem=recv_sem.at[number + turn],
                device_id=near_device(REACH, turn),
                device_id_type=MESH,
            )
            for turn in range(1, GROUPS)
        ]

    def ring_copies(buffer, number):
        def move(owner, part, turn, order):
            piece = buffer.at[owner, pl.ds(part * QUARTER, QUARTER)]
            return pltpu.make_async_remote_copy(
                src_ref=piece,
                dst_ref=piece,
                send_sem=send_sem.at[number + order],
                recv_sem=recv_sem.at[number + order],
                device_id=near_device(REACH, turn),
                device_id_type=MESH,
            )

        right = [move(group, part, 1, part) for part in (0, 1, 2, 3)]
        left = [move(group, part, 3, 4 + part) for part in (2, 3, 0, 1)]
        starts = [copy for pair in zip(right, left) for copy in pair]
        onward = []
        for step in range(2):
            onward.append(move(groups[3], step, 1, 8 + step))
            onward.append(move(groups[1], step + 2, 3, 10 + step))
        return starts, starts[:4], onward, starts[4:] + onward

    def halo_copies(buffer, number):
        return [
            pltpu.make_async_remote_copy(
                src_ref=buffer.at[:, 1],
                dst_ref=buffer.at[:, PX + 1],
                send_sem=send_sem.at[number],
                recv_sem=recv_sem.at[number],
                device_id=near_device(REACH - 1, 0),
                device_id_type=MESH,
            ),
            pltpu.make_async_remote_copy(
                src_ref=buffer.at[:, PX],
                dst_ref=buffer.at[:, 0],
                send_sem=send_sem.at[number + 1],
                recv_sem=recv_sem.at[number + 1],
                device_id=near_device(REACH + 1, 0),
                device_id_type=MESH,
            ),
        ]

    REQ, ROWS, ROWS2, HEAT, HEAT2, TARGET = 0, 1, 2, 3, 4, 5
    HALO, HALO2 = 6, 8
    GATHER, GATHER2, SHARE, SHARE2, VEE, VEE2 = 10, 14, 26, 30, 34, 38

    far_send(req_out, req_in, REQ)
    target_send(TARGET)
    halos = halo_copies(cells, HALO)
    vees = group_copies(lambda turn: own_v.at[turn], lambda turn: all_v.at[turn], VEE)
    gathers = group_copies(
        lambda turn: gathered.at[group], lambda turn: gathered.at[group], GATHER
    )
    for copy in halos + vees + gathers:
        copy.start()

    angle_down = jnp.zeros((SLOT_ALL, NZ), F32)
    angle_over = jnp.zeros((SLOT_ALL, NZ), F32)
    slot_row, slot_lane = iota((SLOT_ALL, NZ), 0), iota((SLOT_ALL, NZ), 1)
    for slot in range(SLOT_ALL):
        angle = angles[grains[slot]]
        angle_down = jnp.where(slot_row == slot, angle, angle_down)
        angle_over = jnp.where(slot_lane == slot, angle, angle_over)
    strength = interface_energy / SLOT_ALL * (0.3 + jnp.abs(jnp.sin(angle_down - angle_over)))
    strength = jnp.where((slot_row != slot_lane) & (slot_lane < SLOT_ALL), strength, 0.0)
    strength = strength.astype(BF16)
    column_sums = jnp.sum(strength.astype(F32), axis=0, keepdims=True)
    own_row = iota((COLS, SLOT_ALL), 0) // PY + group * CH
    choose = jnp.where(own_row == iota((COLS, SLOT_ALL), 1), 1.0, 0.0).astype(BF16)
    tall = dot(choose, strength).astype(BF16)
    wide_shape = (NZ, SLOT_ALL * PY)
    widen = jnp.where(iota(wide_shape, 0) == iota(wide_shape, 1) // PY, 1.0, 0.0).astype(BF16)
    weights = dot(tall, widen)
    weights = jnp.where(iota(wide_shape, 0) % PY == iota(wide_shape, 1) % PY, weights, 0.0)
    weights = weights.astype(BF16)
    for owner in range(GROUPS):
        by_owner[owner] = weights[:, owner * COLS : (owner + 1) * COLS]

    def melt_of(channel):
        return melts[grains[group * CH + channel]]

    def sum_of(channel):
        lanes = iota((1, NZ), 1) == group * CH + channel
        return jnp.sum(jnp.where(lanes, column_sums, 0.0), axis=1, keepdims=True)

    def stencil(buffer, kept):
        @pl.when(tile == 0)
        def _():
            buffer[:, 0] = jnp.zeros((CH, PY, NZ), F32)

        @pl.when(tile == TILES - 1)
        def _():
            buffer[:, PX + 1] = jnp.zeros((CH, PY, NZ), F32)

        def one(channel, total):
            padded = buffer[channel]
            now = padded[1:-1].reshape(COLS, NZ)
            gain = time_step * laplacian(padded)
            gain = gain + (melt_of(channel) * (time_step * drive_gain)) * (now - now * now)
            kept[channel] = now + gain
            rounded = now.astype(BF16).astype(F32)
            return total + (gain - (time_step * sum_of(channel)) * rounded)

        return lax.fori_loop(0, CH, one, jnp.zeros((COLS, NZ), F32))

    def mix(buffer):
        for plane in range(PX):
            right = buffer[:, :, plane].reshape(SLOT_ALL * PY, NZ)
            mixed[:, plane] = dot(weights, right).reshape(CH, PY, NZ)

    for copy in halos:
        copy.wait_recv()
    own_u = stencil(cells, static)

    far_done(req_in, recv_sem, REQ)
    for index in range(BLOCK):
        flat[pl.ds(index * SLOTS, SLOTS), :] = req_in[index]
    asked = flat[pl.ds(0, FAR), :].astype(jnp.int32)
    asked = jnp.concatenate([asked, asked], axis=1)
    serve = jnp.where(asked == iota((FAR, NODES), 1), 1.0, 0.0).astype(BF16)

    def spread_rows(values, out):
        flat[pl.ds(0, FAR), :] = values
        for index in range(BLOCK):
            out[index] = flat[pl.ds(index * SLOTS, SLOTS), :]

    def collect_rows(buffer, kept):
        for index in range(BLOCK):
            kept[0, pl.ds(index * SLOTS, SLOTS), :] = buffer[index]

    serve = tripled(serve)
    spread_rows(dot(serve, cold_parts), rows_out)
    far_send(rows_out, rows_in, ROWS)

    target_done(target_in, recv_sem, TARGET)
    heat_flat[...] = jnp.full((HEAT_PAD, NZ), -1.0, F32)
    for offset in range(NEAR):
        heat_flat[pl.ds(offset * HEAT_SLOTS, HEAT_SLOTS), :] = target_in[offset]
    aims = heat_flat[...].astype(jnp.int32)
    aims = jnp.concatenate([aims, jnp.full((NZ - HEAT_PAD, NZ), -1, jnp.int32)], axis=0)
    low = jnp.where(aims == iota((NZ, NZ), 1), 1.0, 0.0).T
    high = jnp.where(aims == iota((NZ, NZ), 1) + NZ, 1.0, 0.0).T
    scatter = jnp.concatenate([low, high], axis=0)[:, :HEAT_PAD].astype(BF16)
    relay = tripled(dot(serve[:, :NODES], scatter).astype(BF16))
    scatter = tripled(scatter)
    warm_rows = dot(serve, warm_parts)
    heat_flat[...] = jnp.zeros((HEAT_PAD, NZ), F32)

    def arrived_heat(buffer):
        for offset in range(NEAR):
            parts = [buffer[offset * GROUPS + turn] for turn in range(GROUPS)]
            heat_flat[pl.ds(offset * HEAT_SLOTS, HEAT_SLOTS), :] = (parts[0] + parts[1]) + (
                parts[2] + parts[3]
            )
        return heat_flat[...]

    def send_heat(kept, own_part, vee, out, target, number):
        warmed = dot(slot_pick, stacked(kept[0] * vee))
        flat[pl.ds(0, HEAT_PAD), :] = own_part - warmed
        for offset in range(NEAR):
            out[offset] = flat[pl.ds(offset * HEAT_SLOTS, HEAT_SLOTS), :]
        heat_send(out, target, number)

    def share_copies(buffer, number):
        return group_copies(lambda turn: buffer.at[0], lambda turn: buffer.at[turn], number)

    for copy in vees:
        copy.wait_recv()
    vee = (own_v[0] + all_v[1]) + (all_v[2] + all_v[3])
    fixed_heat = dot(pool_pick, stacked(own_u))

    far_done(rows_in, recv_sem, ROWS)
    collect_rows(rows_in, share)
    shares = share_copies(share, SHARE)
    for copy in shares:
        copy.start()
    send_heat(share, fixed_heat, vee, heat_out, heat_in, HEAT)
    for copy in gathers:
        copy.wait_recv()
    mix(gathered)
    for copy in shares:
        copy.wait_recv()

    def all_rows(kept):
        return dot(take_turn, stacked(kept[...].reshape(GROUPS * FAR, NZ)))

    cell_temp = all_rows(share)

    def update(channel, total):
        now = cells[channel, pl.ds(1, PX)].reshape(COLS, NZ)
        change = (time_step * drive_gain) * cell_temp * (now - now * now)
        mixing = mixed[channel].reshape(COLS, NZ)
        new = static[channel] - time_step * mixing - change
        shaped = new.reshape(PX, PY, NZ)
        cells2[channel, pl.ds(1, PX)] = shaped
        gathered2[group, channel] = shaped.astype(BF16)
        return total + (new - new * new)

    total = lax.fori_loop(0, CH, update, jnp.zeros((COLS, NZ), F32))
    ring2 = ring_copies(gathered2, GATHER2)
    for copy in ring2[0][:4]:
        copy.start()
    total = (time_step * drive_gain) * total
    own_v2[...] = dot(give_all, stacked(total)).reshape(GROUPS, FAR, NZ)
    halos2 = halo_copies(cells2, HALO2)
    vees2 = group_copies(lambda turn: own_v2.at[turn], lambda turn: all_v2.at[turn], VEE2)
    for copy in vees2 + halos2 + ring2[0][4:]:
        copy.start()

    heat_done(heat_in, recv_sem, HEAT)
    arrived = arrived_heat(heat_in)
    spread_rows(warm_rows + heat_gain * dot(relay, stacked(arrived)), rows_out2)
    far_send(rows_out2, rows_in2, ROWS2)
    final_temp[...] = conduct(warm + heat_gain * dot(scatter, stacked(arrived)))

    for copy in halos2:
        copy.wait_recv()
    for arrived_copy, onward in zip(ring2[1], ring2[2]):
        arrived_copy.wait_recv()
        onward.start()
    own_u2 = stencil(cells2, static2)
    for copy in vees2:
        copy.wait_recv()
    vee2 = (own_v2[0] + all_v2[1]) + (all_v2[2] + all_v2[3])
    fixed_heat2 = dot(pool_pick, stacked(own_u2))

    far_done(rows_in2, recv_sem, ROWS2)
    collect_rows(rows_in2, share2)
    send_heat(share2, fixed_heat2, vee2, heat_out2, heat_in2, HEAT2)
    shares2 = share_copies(share2, SHARE2)
    for copy in shares2:
        copy.start()

    for copy in ring2[3][:4]:
        copy.wait_recv()

    def block_of(owner, plane):
        right = gathered2[owner, :, plane].reshape(COLS, NZ)
        return dot(by_owner[owner], right).reshape(CH, PY, NZ)

    for plane in range(PX):
        mixed[:, plane] = block_of(group, plane) + (
            block_of(groups[1], plane) + block_of(groups[3], plane)
        )
    for copy in ring2[3][4:]:
        copy.wait_recv()
    for plane in range(PX):
        mixed[:, plane] += block_of(groups[2], plane)
    for copy in shares2:
        copy.wait_recv()
    cell_temp2 = all_rows(share2)

    stores = []
    for channel in range(CH):
        now = cells2[channel, pl.ds(1, PX)].reshape(COLS, NZ)
        change = (time_step * drive_gain) * cell_temp2 * (now - now * now)
        mixing = mixed[channel].reshape(COLS, NZ)
        static2[channel] = static2[channel] - time_step * mixing - change
        store = pltpu.make_async_copy(
            static2.at[channel], phases_out.at[channel], load_sem.at[channel]
        )
        store.start()
        stores.append(store)

    heat_done(heat_in2, recv_sem, HEAT2)
    arrived = arrived_heat(heat_in2)
    final_temp[...] = final_temp[...] + heat_gain * dot(scatter, stacked(arrived))
    store_temp = pltpu.make_async_copy(final_temp, temp_out, load_sem.at[CH])
    store_temp.start()

    far_done(req_out, send_sem, REQ)
    far_done(rows_out, send_sem, ROWS)
    far_done(rows_out2, send_sem, ROWS2)
    heat_done(heat_in, send_sem, HEAT)
    heat_done(heat_in2, send_sem, HEAT2)
    target_done(target_out, send_sem, TARGET)
    for copy in halos + vees + gathers + shares + halos2 + vees2 + ring2[0] + ring2[2] + shares2:
        copy.wait_send()
    for store in stores + [store_temp]:
        store.wait()


def place_results(new, temp, new_out, temp_out):
    new_out[...] = new[...]
    temp_out[...] = temp[...]


def on_device(
    phases, node_temp, column_nodes, grain_ids, grain_angle, grain_melt, heat_owner, heat_local
):
    outside = pl.BlockSpec(memory_space=pl.ANY)
    vmem, smem = pltpu.VMEM, pltpu.SMEM
    gathered = vmem((GROUPS, CH, PX, PY, NZ), BF16)
    padded = vmem((CH, PX + 2, PY, NZ), F32)
    flat_cells = vmem((CH, COLS, NZ), F32)
    mix_out = vmem((CH, PX, PY, NZ), F32)
    far_rows = vmem((BLOCK, SLOTS, NZ), F32)
    shared = vmem((GROUPS, FAR, NZ), F32)
    heat_out = vmem((NEAR, HEAT_SLOTS, NZ), F32)
    heat_in = vmem((NEAR * GROUPS, HEAT_SLOTS, NZ), F32)
    new, temp = pl.pallas_call(
        kernel,
        out_shape=(
            jax.ShapeDtypeStruct((CH, COLS, NZ), F32),
            jax.ShapeDtypeStruct(node_temp.shape, F32),
        ),
        in_specs=[outside] * 8,
        out_specs=(outside, outside),
        scratch_shapes=[
            padded, padded, flat_cells, flat_cells, mix_out, gathered, gathered,
            vmem((NODES, NZ), F32), vmem((1, COLS), jnp.int32), smem((SLOT_ALL,), jnp.int32),
            smem((grain_angle.shape[0],), F32), smem((grain_melt.shape[0],), F32),
            smem((POOL,), jnp.int32), smem((POOL,), jnp.int32),
            far_rows, far_rows, far_rows, far_rows, far_rows, far_rows, shared, shared,
            heat_out, heat_in, heat_out, heat_in, heat_out, heat_out,
            shared, shared, shared, shared, vmem((GROUPS, COLS, COLS), BF16), vmem((FAR, NZ), F32), vmem((HEAT_PAD, NZ), F32),
            vmem((NODES, NZ), F32),
            pltpu.SemaphoreType.DMA((CH + 1,)),
            pltpu.SemaphoreType.DMA((42,)),
            pltpu.SemaphoreType.DMA((42,)),
        ],
        compiler_params=pltpu.CompilerParams(
            collective_id=0, has_side_effects=True, vmem_limit_bytes=56 << 20
        ),
        name="solidify",
    )(
        phases,
        node_temp,
        column_nodes.reshape(1, COLS),
        grain_ids.reshape(SLOT_ALL),
        grain_angle,
        grain_melt,
        heat_owner.reshape(POOL),
        heat_local,
    )
    halves = (
        pl.BlockSpec((CH // 2, COLS, NZ), lambda half: (half, 0, 0)),
        pl.BlockSpec((NODES // 2, NZ), lambda half: (half, 0)),
    )
    placed, temp = pl.pallas_call(
        place_results,
        out_shape=(
            jax.ShapeDtypeStruct(new.shape, F32),
            jax.ShapeDtypeStruct(temp.shape, F32),
        ),
        grid=(2,),
        in_specs=halves,
        out_specs=halves,
        name="results",
    )(new, temp)
    return placed.reshape(phases.shape), temp


def solution(mesh):
    placed = (
        P("ch", "tile", None, None),
        P("tile", None),
        P("tile"),
        P("tile", None),
        P(),
        P(),
        P("tile", None),
        P("tile"),
    )
    return jax.shard_map(
        on_device,
        mesh=mesh,
        in_specs=placed,
        out_specs=(P("ch", "tile", None, None), P("tile", None)),
        check_vma=False,
    )
```

```python
import functools

import jax
import jax.numpy as jnp
from jax import lax
from jax.experimental import pallas as pl
from jax.experimental.pallas import tpu as pltpu
from jax.sharding import PartitionSpec as P

STEPS = 2
MESH = pl.DeviceIdType.MESH
F32 = jnp.float32
BF16 = jnp.bfloat16

time_step = 0.1
interface_energy = 1.0
drive_gain = 3.0
heat_gain = 0.5
depth_diffusion = 0.2

TILES = 128
GROUPS = 4
BLOCK = TILES // GROUPS
SLOTS = 2
REACH = 3
NEAR = 2 * REACH + 1
HEAT_SLOTS = 4
CH = 8
SLOT_ALL = 32
PX = 8
PY = 16
NZ = 128
COLS = PX * PY
NODES = 256
POOL = 16
FAR = BLOCK * SLOTS
HEAT_ROWS = NEAR * HEAT_SLOTS
HEAT_PAD = 32
QUARTER = CH // 4


def iota(shape, dim):
    return lax.broadcasted_iota(jnp.int32, shape, dim)


def dot(a, b):
    return jnp.dot(a, b, preferred_element_type=F32)


def thirds(value):
    high = value.astype(BF16)
    rest = value - high.astype(F32)
    mid = rest.astype(BF16)
    low = (rest - mid.astype(F32)).astype(BF16)
    return high, mid, low


def stacked(value):
    return jnp.concatenate(thirds(value), axis=0)


def tripled(onehot):
    return jnp.concatenate([onehot, onehot, onehot], axis=1)


def beside(values):
    rows, lanes = values.shape
    lane = iota((rows, lanes), 1)
    up = jnp.where(lane == lanes - 1, 0.0, pltpu.roll(values, lanes - 1, 1))
    down = jnp.where(lane == 0, 0.0, pltpu.roll(values, 1, 1))
    return up + down


def across(values):
    rows, lanes = values.shape
    place = iota((rows, lanes), 0) % PY
    up = jnp.where(place == PY - 1, 0.0, pltpu.roll(values, rows - 1, 0))
    down = jnp.where(place == 0, 0.0, pltpu.roll(values, 1, 0))
    return up + down


def laplacian(padded):
    flat = padded.reshape((PX + 2) * PY, NZ)
    along_y = across(flat)
    inner = (6.0 * along_y - 88.0 * flat) + beside(6.0 * flat + 3.0 * along_y)
    outer = (6.0 * flat + 3.0 * along_y) + beside(3.0 * flat + 2.0 * along_y)
    total = inner[PY:-PY] + (outer[2 * PY :] + outer[: -2 * PY])
    return total * (1.0 / 26.0)


def conduct(rows):
    lane = iota(rows.shape, 1)
    up = jnp.where(lane == NZ - 1, rows, pltpu.roll(rows, NZ - 1, 1))
    down = jnp.where(lane == 0, rows, pltpu.roll(rows, 1, 1))
    return rows + depth_diffusion * (up - 2.0 * rows + down)


def kernel(
    phases_hbm, temp_hbm, columns_hbm, grains_hbm, angle_hbm, melt_hbm, owner_hbm, local_hbm,
    phases_out, temp_out,
    cells, cells2, static, static2, mixed, gathered, gathered2,
    temp, columns, grains, angles, melts, owners, locals_,
    req_out, req_in, rows_out, rows_in, rows_out2, rows_in2, share, share2,
    heat_out, heat_in, heat_out2, heat_in2, target_out, target_in,
    own_v, own_v2, all_v, all_v2, by_owner, flat, heat_flat, final_temp,
    load_sem, send_sem, recv_sem,
):
    tile = lax.axis_index("tile")
    group = lax.axis_index("ch")
    block = tile // BLOCK
    place = tile % BLOCK
    partner = (group + GROUPS - block) % GROUPS
    inside = partner == block

    first = partner * BLOCK
    near_tiles = [lax.rem(tile + (TILES + step - REACH), TILES) for step in range(NEAR)]
    groups = [group] + [lax.rem(group + turn, GROUPS) for turn in range(1, GROUPS)]
    near_order = [
        (offset, turn) for turn in (2, 1, 3, 0) for offset in (0, 6, 1, 5, 2, 4, 3)
    ][:-1]

    def far_index(number):
        half = (number + 1) // 2
        turn = jnp.where(number % 2 == 0, half, BLOCK - half)
        return lax.rem(place + BLOCK // 2 + turn, BLOCK)

    def far_device(index):
        return {"tile": first + index, "ch": group}

    def near_device(offset, turn):
        return {"tile": near_tiles[offset], "ch": groups[turn]}

    barrier = pltpu.get_barrier_semaphore()

    def greet_far(number, _):
        pl.semaphore_signal(
            barrier, inc=1, device_id=far_device(far_index(number)), device_id_type=MESH
        )
        return 0

    lax.fori_loop(0, BLOCK - 1, greet_far, 0)

    @pl.when(jnp.logical_not(inside))
    def _():
        greet_far(BLOCK - 1, 0)

    for offset, turn in near_order:
        pl.semaphore_signal(
            barrier, inc=1, device_id=near_device(offset, turn), device_id_type=MESH
        )

    loads = [
        pltpu.make_async_copy(phases_hbm, cells.at[:, pl.ds(1, PX)], load_sem.at[0]),
        pltpu.make_async_copy(temp_hbm, temp, load_sem.at[1]),
        pltpu.make_async_copy(columns_hbm, columns, load_sem.at[2]),
        pltpu.make_async_copy(grains_hbm, grains, load_sem.at[3]),
        pltpu.make_async_copy(angle_hbm, angles, load_sem.at[4]),
        pltpu.make_async_copy(melt_hbm, melts, load_sem.at[5]),
        pltpu.make_async_copy(owner_hbm, owners, load_sem.at[6]),
        pltpu.make_async_copy(local_hbm, locals_, load_sem.at[7]),
    ]
    for load in loads:
        load.start()
    loads[2].wait()

    wanted = jnp.broadcast_to(columns[...].astype(F32), (COLS, COLS))
    wanted_down = wanted.T
    wanted_i = wanted.astype(jnp.int32)
    wanted_down_i = wanted_down.astype(jnp.int32)
    owner_over = wanted_i // NODES
    owner_down = wanted_down_i // NODES
    local_down = (wanted_down_i % NODES).astype(F32)
    down, over = iota((COLS, COLS), 0), iota((COLS, COLS), 1)
    same = owner_over == owner_down
    slot_over = jnp.sum(jnp.where(same & (down < over), 1.0, 0.0), axis=0, keepdims=True)
    slot_down = jnp.sum(jnp.where(same & (over < down), 1.0, 0.0), axis=1, keepdims=True)
    key_over = owner_over[:1] * SLOTS + slot_over.astype(jnp.int32)
    key_down = owner_down[:, :1] * SLOTS + slot_down.astype(jnp.int32)
    ask = jnp.where(iota((FAR, COLS), 0) + partner * FAR == key_over, 1.0, 0.0).astype(BF16)
    flat[pl.ds(0, FAR), :] = dot(ask, local_down.astype(BF16))
    for index in range(BLOCK):
        req_out[index] = flat[pl.ds(index * SLOTS, SLOTS), :]
    pl.semaphore_wait(
        barrier, NEAR * GROUPS - 1 + jnp.where(inside, BLOCK - 1, BLOCK).astype(jnp.int32)
    )

    def far_copy(source, target, index, number):
        return pltpu.make_async_remote_copy(
            src_ref=source.at[index],
            dst_ref=target.at[place],
            send_sem=send_sem.at[number],
            recv_sem=recv_sem.at[number],
            device_id=far_device(index),
            device_id_type=MESH,
        )

    def far_send(source, target, number):
        def one(order, _):
            far_copy(source, target, far_index(order), number).start()
            return 0

        lax.fori_loop(0, BLOCK - 1, one, 0)

        @pl.when(jnp.logical_not(inside))
        def _():
            one(BLOCK - 1, 0)

        @pl.when(inside)
        def _():
            target[place] = source[place]

    def far_done(buffer, sem, number):
        @pl.when(inside)
        def _():
            part = buffer.at[pl.ds(0, BLOCK - 1)]
            pltpu.make_async_copy(part, part, sem.at[number]).wait()

        @pl.when(jnp.logical_not(inside))
        def _():
            pltpu.make_async_copy(buffer, buffer, sem.at[number]).wait()

    def heat_send(source, target, number):
        for offset, turn in near_order:
            pltpu.make_async_remote_copy(
                src_ref=source.at[offset],
                dst_ref=target.at[offset * GROUPS + group],
                send_sem=send_sem.at[number],
                recv_sem=recv_sem.at[number],
                device_id=near_device(offset, turn),
                device_id_type=MESH,
            ).start()
        target[REACH * GROUPS + group] = source[REACH]

    def heat_done(buffer, sem, number):
        part = buffer.at[pl.ds(0, NEAR * GROUPS - 1)]
        pltpu.make_async_copy(part, part, sem.at[number]).wait()

    def target_send(number):
        for offset in (0, 6, 1, 5, 2, 4):
            pltpu.make_async_remote_copy(
                src_ref=target_out.at[offset],
                dst_ref=target_in.at[offset],
                send_sem=send_sem.at[number],
                recv_sem=recv_sem.at[number],
                device_id=near_device(offset, 0),
                device_id_type=MESH,
            ).start()
        target_in[REACH] = target_out[REACH]

    def target_done(buffer, sem, number):
        part = buffer.at[pl.ds(0, NEAR - 1)]
        pltpu.make_async_copy(part, part, sem.at[number]).wait()

    def group_copies(source_of, target_of, number):
        return [
            pltpu.make_async_remote_copy(
                src_ref=source_of(turn),
                dst_ref=target_of(turn),
                send_sem=send_sem.at[number + turn],
                recv_sem=recv_sem.at[number + turn],
                device_id=near_device(REACH, turn),
                device_id_type=MESH,
            )
            for turn in range(1, GROUPS)
        ]

    def ring_copies(buffer, number):
        def move(owner, part, turn, order):
            piece = buffer.at[owner, pl.ds(part * QUARTER, QUARTER)]
            return pltpu.make_async_remote_copy(
                src_ref=piece,
                dst_ref=piece,
                send_sem=send_sem.at[number + order],
                recv_sem=recv_sem.at[number + order],
                device_id=near_device(REACH, turn),
                device_id_type=MESH,
            )

        right = [move(group, part, 1, part) for part in (0, 1, 2, 3)]
        left = [move(group, part, 3, 4 + part) for part in (2, 3, 0, 1)]
        starts = [copy for pair in zip(right, left) for copy in pair]
        onward = []
        for step in range(2):
            onward.append(move(groups[3], step, 1, 8 + step))
            onward.append(move(groups[1], step + 2, 3, 10 + step))
        return starts, starts[:4], onward, starts[4:] + onward

    def halo_copies(buffer, number):
        return [
            pltpu.make_async_remote_copy(
                src_ref=buffer.at[:, 1],
                dst_ref=buffer.at[:, PX + 1],
                send_sem=send_sem.at[number],
                recv_sem=recv_sem.at[number],
                device_id=near_device(REACH - 1, 0),
                device_id_type=MESH,
            ),
            pltpu.make_async_remote_copy(
                src_ref=buffer.at[:, PX],
                dst_ref=buffer.at[:, 0],
                send_sem=send_sem.at[number + 1],
                recv_sem=recv_sem.at[number + 1],
                device_id=near_device(REACH + 1, 0),
                device_id_type=MESH,
            ),
        ]

    REQ, ROWS, ROWS2, HEAT, HEAT2, TARGET = 0, 1, 2, 3, 4, 5
    HALO, HALO2 = 6, 8
    GATHER, GATHER2, SHARE, SHARE2, VEE, VEE2 = 10, 14, 26, 30, 34, 38

    far_send(req_out, req_in, REQ)

    for load in loads[:2] + loads[3:]:
        load.wait()

    key_lane = iota((COLS, FAR), 1)
    take_own = jnp.where(key_lane + partner * FAR == key_down, 1.0, 0.0).astype(BF16)
    row_all = iota((GROUPS * FAR, COLS), 0)
    row_block = ((group + row_all // FAR) % GROUPS + GROUPS - block) % GROUPS
    give_all = jnp.where(row_block * FAR + row_all % FAR == key_over, 1.0, 0.0).astype(BF16)
    give_all = tripled(give_all)
    lane_all = iota((COLS, GROUPS * FAR), 1)
    lane_group = (group + GROUPS - lane_all // FAR) % GROUPS
    lane_block = (lane_group + GROUPS - block) % GROUPS
    take_turn = jnp.where(
        lane_block * FAR + lane_all % FAR == key_down, 1.0, 0.0
    ).astype(BF16)
    take_turn = tripled(take_turn)

    row_down, lane = iota((POOL, COLS), 0), iota((POOL, COLS), 1)
    off_down = jnp.zeros((POOL, COLS), jnp.int32)
    off_over = jnp.zeros((POOL, COLS), jnp.int32)
    local_rows = jnp.zeros((POOL, NZ), jnp.int32)
    for row in range(POOL):
        off = (owners[row] - tile + (REACH + TILES)) % TILES
        off_down = jnp.where(row_down == row, off, off_down)
        off_over = jnp.where(lane // 8 == row, off, off_over)
        local_rows = jnp.where(row_down == row, locals_[row], local_rows)
    earlier = jnp.where((off_down == off_over) & (row_down < lane // 8), 1.0, 0.0)
    heat_slot = jnp.sum(earlier, axis=0, keepdims=True).astype(jnp.int32)
    heat_key = off_over[:1] * HEAT_SLOTS + heat_slot
    spread = iota((HEAT_PAD, COLS), 0) == heat_key
    pool_pick = jnp.where(spread, 1.0, 0.0).astype(BF16)
    row_of = jnp.where(iota((COLS, POOL), 0) == 8 * iota((COLS, POOL), 1), 1.0, 0.0).astype(BF16)
    row_pick = dot(pool_pick, row_of).astype(BF16)
    slot_pick = tripled(dot(pool_pick, take_own).astype(BF16))
    pool_pick = tripled(pool_pick)
    flat[pl.ds(0, HEAT_PAD), :] = dot(row_pick, local_rows.astype(F32).astype(BF16))
    for offset in range(NEAR):
        target_out[offset] = flat[pl.ds(offset * HEAT_SLOTS, HEAT_SLOTS), :]

    def first_look(channel, total):
        now = cells[channel, pl.ds(1, PX)]
        gathered[group, channel] = now.astype(BF16)
        return total + (now - now * now)

    total = lax.fori_loop(0, CH, first_look, jnp.zeros((PX, PY, NZ), F32))
    total = (time_step * drive_gain) * total.reshape(COLS, NZ)
    own_v[...] = dot(give_all, stacked(total)).reshape(GROUPS, FAR, NZ)

    warm = conduct(temp[...])
    cold_parts, warm_parts = stacked(temp[...]), stacked(warm)
    target_send(TARGET)
    halos = halo_copies(cells, HALO)
    vees = group_copies(lambda turn: own_v.at[turn], lambda turn: all_v.at[turn], VEE)
    gathers = group_copies(
        lambda turn: gathered.at[group], lambda turn: gathered.at[group], GATHER
    )
    for copy in halos + vees + gathers:
        copy.start()

    angle_down = jnp.zeros((SLOT_ALL, NZ), F32)
    angle_over = jnp.zeros((SLOT_ALL, NZ), F32)
    slot_row, slot_lane = iota((SLOT_ALL, NZ), 0), iota((SLOT_ALL, NZ), 1)
    for slot in range(SLOT_ALL):
        angle = angles[grains[slot]]
        angle_down = jnp.where(slot_row == slot, angle, angle_down)
        angle_over = jnp.where(slot_lane == slot, angle, angle_over)
    strength = interface_energy / SLOT_ALL * (0.3 + jnp.abs(jnp.sin(angle_down - angle_over)))
    strength = jnp.where((slot_row != slot_lane) & (slot_lane < SLOT_ALL), strength, 0.0)
    strength = strength.astype(BF16)
    column_sums = jnp.sum(strength.astype(F32), axis=0, keepdims=True)
    own_row = iota((COLS, SLOT_ALL), 0) // PY + group * CH
    choose = jnp.where(own_row == iota((COLS, SLOT_ALL), 1), 1.0, 0.0).astype(BF16)
    tall = dot(choose, strength).astype(BF16)
    wide_shape = (NZ, SLOT_ALL * PY)
    widen = jnp.where(iota(wide_shape, 0) == iota(wide_shape, 1) // PY, 1.0, 0.0).astype(BF16)
    weights = dot(tall, widen)
    weights = jnp.where(iota(wide_shape, 0) % PY == iota(wide_shape, 1) % PY, weights, 0.0)
    weights = weights.astype(BF16)
    for owner in range(GROUPS):
        by_owner[owner] = weights[:, owner * COLS : (owner + 1) * COLS]

    def melt_of(channel):
        return melts[grains[group * CH + channel]]

    def sum_of(channel):
        lanes = iota((1, NZ), 1) == group * CH + channel
        return jnp.sum(jnp.where(lanes, column_sums, 0.0), axis=1, keepdims=True)

    def stencil(buffer, kept):
        @pl.when(tile == 0)
        def _():
            buffer[:, 0] = jnp.zeros((CH, PY, NZ), F32)

        @pl.when(tile == TILES - 1)
        def _():
            buffer[:, PX + 1] = jnp.zeros((CH, PY, NZ), F32)

        def one(channel, total):
            padded = buffer[channel]
            now = padded[1:-1].reshape(COLS, NZ)
            gain = time_step * laplacian(padded)
            gain = gain + (melt_of(channel) * (time_step * drive_gain)) * (now - now * now)
            kept[channel] = now + gain
            rounded = now.astype(BF16).astype(F32)
            return total + (gain - (time_step * sum_of(channel)) * rounded)

        return lax.fori_loop(0, CH, one, jnp.zeros((COLS, NZ), F32))

    def mix(buffer):
        for plane in range(PX):
            right = buffer[:, :, plane].reshape(SLOT_ALL * PY, NZ)
            mixed[:, plane] = dot(weights, right).reshape(CH, PY, NZ)

    for copy in halos:
        copy.wait_recv()
    own_u = stencil(cells, static)

    far_done(req_in, recv_sem, REQ)
    for index in range(BLOCK):
        flat[pl.ds(index * SLOTS, SLOTS), :] = req_in[index]
    asked = flat[pl.ds(0, FAR), :].astype(jnp.int32)
    asked = jnp.concatenate([asked, asked], axis=1)
    serve = jnp.where(asked == iota((FAR, NODES), 1), 1.0, 0.0).astype(BF16)

    def spread_rows(values, out):
        flat[pl.ds(0, FAR), :] = values
        for index in range(BLOCK):
            out[index] = flat[pl.ds(index * SLOTS, SLOTS), :]

    def collect_rows(buffer, kept):
        for index in range(BLOCK):
            kept[0, pl.ds(index * SLOTS, SLOTS), :] = buffer[index]

    serve = tripled(serve)
    spread_rows(dot(serve, cold_parts), rows_out)
    far_send(rows_out, rows_in, ROWS)

    target_done(target_in, recv_sem, TARGET)
    heat_flat[...] = jnp.full((HEAT_PAD, NZ), -1.0, F32)
    for offset in range(NEAR):
        heat_flat[pl.ds(offset * HEAT_SLOTS, HEAT_SLOTS), :] = target_in[offset]
    aims = heat_flat[...].astype(jnp.int32)
    aims = jnp.concatenate([aims, jnp.full((NZ - HEAT_PAD, NZ), -1, jnp.int32)], axis=0)
    low = jnp.where(aims == iota((NZ, NZ), 1), 1.0, 0.0).T
    high = jnp.where(aims == iota((NZ, NZ), 1) + NZ, 1.0, 0.0).T
    scatter = jnp.concatenate([low, high], axis=0)[:, :HEAT_PAD].astype(BF16)
    relay = tripled(dot(serve[:, :NODES], scatter).astype(BF16))
    scatter = tripled(scatter)
    warm_rows = dot(serve, warm_parts)
    heat_flat[...] = jnp.zeros((HEAT_PAD, NZ), F32)

    def arrived_heat(buffer):
        for offset in range(NEAR):
            parts = [buffer[offset * GROUPS + turn] for turn in range(GROUPS)]
            heat_flat[pl.ds(offset * HEAT_SLOTS, HEAT_SLOTS), :] = (parts[0] + parts[1]) + (
                parts[2] + parts[3]
            )
        return heat_flat[...]

    def send_heat(kept, own_part, vee, out, target, number):
        warmed = dot(slot_pick, stacked(kept[0] * vee))
        flat[pl.ds(0, HEAT_PAD), :] = own_part - warmed
        for offset in range(NEAR):
            out[offset] = flat[pl.ds(offset * HEAT_SLOTS, HEAT_SLOTS), :]
        heat_send(out, target, number)

    def share_copies(buffer, number):
        return group_copies(lambda turn: buffer.at[0], lambda turn: buffer.at[turn], number)

    for copy in vees:
        copy.wait_recv()
    vee = (own_v[0] + all_v[1]) + (all_v[2] + all_v[3])
    fixed_heat = dot(pool_pick, stacked(own_u))

    far_done(rows_in, recv_sem, ROWS)
    collect_rows(rows_in, share)
    shares = share_copies(share, SHARE)
    for copy in shares:
        copy.start()
    send_heat(share, fixed_heat, vee, heat_out, heat_in, HEAT)
    for copy in gathers:
        copy.wait_recv()
    mix(gathered)
    for copy in shares:
        copy.wait_recv()

    def all_rows(kept):
        return dot(take_turn, stacked(kept[...].reshape(GROUPS * FAR, NZ)))

    cell_temp = all_rows(share)

    def update(channel, total):
        now = cells[channel, pl.ds(1, PX)].reshape(COLS, NZ)
        change = (time_step * drive_gain) * cell_temp * (now - now * now)
        mixing = mixed[channel].reshape(COLS, NZ)
        new = static[channel] - time_step * mixing - change
        shaped = new.reshape(PX, PY, NZ)
        cells2[channel, pl.ds(1, PX)] = shaped
        gathered2[group, channel] = shaped.astype(BF16)
        return total + (new - new * new)

    total = lax.fori_loop(0, CH, update, jnp.zeros((COLS, NZ), F32))
    ring2 = ring_copies(gathered2, GATHER2)
    for copy in ring2[0][:4]:
        copy.start()
    total = (time_step * drive_gain) * total
    own_v2[...] = dot(give_all, stacked(total)).reshape(GROUPS, FAR, NZ)
    halos2 = halo_copies(cells2, HALO2)
    vees2 = group_copies(lambda turn: own_v2.at[turn], lambda turn: all_v2.at[turn], VEE2)
    for copy in vees2 + halos2 + ring2[0][4:]:
        copy.start()

    heat_done(heat_in, recv_sem, HEAT)
    arrived = arrived_heat(heat_in)
    spread_rows(warm_rows + heat_gain * dot(relay, stacked(arrived)), rows_out2)
    far_send(rows_out2, rows_in2, ROWS2)
    final_temp[...] = conduct(warm + heat_gain * dot(scatter, stacked(arrived)))

    for copy in halos2:
        copy.wait_recv()
    for arrived_copy, onward in zip(ring2[1], ring2[2]):
        arrived_copy.wait_recv()
        onward.start()
    own_u2 = stencil(cells2, static2)
    for copy in vees2:
        copy.wait_recv()
    vee2 = (own_v2[0] + all_v2[1]) + (all_v2[2] + all_v2[3])
    fixed_heat2 = dot(pool_pick, stacked(own_u2))

    far_done(rows_in2, recv_sem, ROWS2)
    collect_rows(rows_in2, share2)
    send_heat(share2, fixed_heat2, vee2, heat_out2, heat_in2, HEAT2)
    shares2 = share_copies(share2, SHARE2)
    for copy in shares2:
        copy.start()

    for copy in ring2[3][:4]:
        copy.wait_recv()

    def block_of(owner, plane):
        right = gathered2[owner, :, plane].reshape(COLS, NZ)
        return dot(by_owner[owner], right).reshape(CH, PY, NZ)

    for plane in range(PX):
        mixed[:, plane] = block_of(group, plane) + (
            block_of(groups[1], plane) + block_of(groups[3], plane)
        )
    for copy in ring2[3][4:]:
        copy.wait_recv()
    for plane in range(PX):
        mixed[:, plane] += block_of(groups[2], plane)
    for copy in shares2:
        copy.wait_recv()
    cell_temp2 = all_rows(share2)

    stores = []
    for channel in range(CH):
        now = cells2[channel, pl.ds(1, PX)].reshape(COLS, NZ)
        change = (time_step * drive_gain) * cell_temp2 * (now - now * now)
        mixing = mixed[channel].reshape(COLS, NZ)
        static2[channel] = static2[channel] - time_step * mixing - change
        store = pltpu.make_async_copy(
            static2.at[channel], phases_out.at[channel], load_sem.at[channel]
        )
        store.start()
        stores.append(store)

    heat_done(heat_in2, recv_sem, HEAT2)
    arrived = arrived_heat(heat_in2)
    final_temp[...] = final_temp[...] + heat_gain * dot(scatter, stacked(arrived))
    store_temp = pltpu.make_async_copy(final_temp, temp_out, load_sem.at[CH])
    store_temp.start()

    far_done(req_out, send_sem, REQ)
    far_done(rows_out, send_sem, ROWS)
    far_done(rows_out2, send_sem, ROWS2)
    heat_done(heat_in, send_sem, HEAT)
    heat_done(heat_in2, send_sem, HEAT2)
    target_done(target_out, send_sem, TARGET)
    for copy in halos + vees + gathers + shares + halos2 + vees2 + ring2[0] + ring2[2] + shares2:
        copy.wait_send()
    for store in stores + [store_temp]:
        store.wait()


def place_results(new, temp, new_out, temp_out):
    new_out[...] = new[...]
    temp_out[...] = temp[...]


def on_device(
    phases, node_temp, column_nodes, grain_ids, grain_angle, grain_melt, heat_owner, heat_local
):
    outside = pl.BlockSpec(memory_space=pl.ANY)
    vmem, smem = pltpu.VMEM, pltpu.SMEM
    gathered = vmem((GROUPS, CH, PX, PY, NZ), BF16)
    padded = vmem((CH, PX + 2, PY, NZ), F32)
    flat_cells = vmem((CH, COLS, NZ), F32)
    mix_out = vmem((CH, PX, PY, NZ), F32)
    far_rows = vmem((BLOCK, SLOTS, NZ), F32)
    shared = vmem((GROUPS, FAR, NZ), F32)
    heat_out = vmem((NEAR, HEAT_SLOTS, NZ), F32)
    heat_in = vmem((NEAR * GROUPS, HEAT_SLOTS, NZ), F32)
    new, temp = pl.pallas_call(
        kernel,
        out_shape=(
            jax.ShapeDtypeStruct((CH, COLS, NZ), F32),
            jax.ShapeDtypeStruct(node_temp.shape, F32),
        ),
        in_specs=[outside] * 8,
        out_specs=(outside, outside),
        scratch_shapes=[
            padded, padded, flat_cells, flat_cells, mix_out, gathered, gathered,
            vmem((NODES, NZ), F32), vmem((1, COLS), jnp.int32), smem((SLOT_ALL,), jnp.int32),
            smem((grain_angle.shape[0],), F32), smem((grain_melt.shape[0],), F32),
            smem((POOL,), jnp.int32), smem((POOL,), jnp.int32),
            far_rows, far_rows, far_rows, far_rows, far_rows, far_rows, shared, shared,
            heat_out, heat_in, heat_out, heat_in, heat_out, heat_out,
            shared, shared, shared, shared, vmem((GROUPS, COLS, COLS), BF16), vmem((FAR, NZ), F32), vmem((HEAT_PAD, NZ), F32),
            vmem((NODES, NZ), F32),
            pltpu.SemaphoreType.DMA((CH + 1,)),
            pltpu.SemaphoreType.DMA((42,)),
            pltpu.SemaphoreType.DMA((42,)),
        ],
        compiler_params=pltpu.CompilerParams(
            collective_id=0, has_side_effects=True, vmem_limit_bytes=56 << 20
        ),
        name="solidify",
    )(
        phases,
        node_temp,
        column_nodes.reshape(1, COLS),
        grain_ids.reshape(SLOT_ALL),
        grain_angle,
        grain_melt,
        heat_owner.reshape(POOL),
        heat_local,
    )
    halves = (
        pl.BlockSpec((CH // 2, COLS, NZ), lambda half: (half, 0, 0)),
        pl.BlockSpec((NODES // 2, NZ), lambda half: (half, 0)),
    )
    placed, temp = pl.pallas_call(
        place_results,
        out_shape=(
            jax.ShapeDtypeStruct(new.shape, F32),
            jax.ShapeDtypeStruct(temp.shape, F32),
        ),
        grid=(2,),
        in_specs=halves,
        out_specs=halves,
        name="results",
    )(new, temp)
    return placed.reshape(phases.shape), temp


def solution(mesh):
    placed = (
        P("ch", "tile", None, None),
        P("tile", None),
        P("tile"),
        P("tile", None),
        P(),
        P(),
        P("tile", None),
        P("tile"),
    )
    return jax.shard_map(
        on_device,
        mesh=mesh,
        in_specs=placed,
        out_specs=(P("ch", "tile", None, None), P("tile", None)),
        check_vma=False,
    )
```

```python
import functools

import jax
import jax.numpy as jnp
from jax import lax
from jax.experimental import pallas as pl
from jax.experimental.pallas import tpu as pltpu
from jax.sharding import PartitionSpec as P

STEPS = 2
MESH = pl.DeviceIdType.MESH
F32 = jnp.float32
BF16 = jnp.bfloat16

time_step = 0.1
interface_energy = 1.0
drive_gain = 3.0
heat_gain = 0.5
depth_diffusion = 0.2

TILES = 128
GROUPS = 4
BLOCK = TILES // GROUPS
SLOTS = 2
REACH = 3
NEAR = 2 * REACH + 1
HEAT_SLOTS = 4
CH = 8
SLOT_ALL = 32
PX = 8
PY = 16
NZ = 128
COLS = PX * PY
NODES = 256
POOL = 16
FAR = BLOCK * SLOTS
HEAT_ROWS = NEAR * HEAT_SLOTS
HEAT_PAD = 32
QUARTER = CH // 4


def iota(shape, dim):
    return lax.broadcasted_iota(jnp.int32, shape, dim)


def dot(a, b):
    return jnp.dot(a, b, preferred_element_type=F32)


def thirds(value):
    high = value.astype(BF16)
    rest = value - high.astype(F32)
    mid = rest.astype(BF16)
    low = (rest - mid.astype(F32)).astype(BF16)
    return high, mid, low


def stacked(value):
    return jnp.concatenate(thirds(value), axis=0)


def tripled(onehot):
    return jnp.concatenate([onehot, onehot, onehot], axis=1)


def beside(values):
    rows, lanes = values.shape
    lane = iota((rows, lanes), 1)
    up = jnp.where(lane == lanes - 1, 0.0, pltpu.roll(values, lanes - 1, 1))
    down = jnp.where(lane == 0, 0.0, pltpu.roll(values, 1, 1))
    return up + down


def across(values):
    rows, lanes = values.shape
    place = iota((rows, lanes), 0) % PY
    up = jnp.where(place == PY - 1, 0.0, pltpu.roll(values, rows - 1, 0))
    down = jnp.where(place == 0, 0.0, pltpu.roll(values, 1, 0))
    return up + down


def laplacian(padded):
    flat = padded.reshape((PX + 2) * PY, NZ)
    along_y = across(flat)
    inner = (6.0 * along_y - 88.0 * flat) + beside(6.0 * flat + 3.0 * along_y)
    outer = (6.0 * flat + 3.0 * along_y) + beside(3.0 * flat + 2.0 * along_y)
    total = inner[PY:-PY] + (outer[2 * PY :] + outer[: -2 * PY])
    return total * (1.0 / 26.0)


def conduct(rows):
    lane = iota(rows.shape, 1)
    up = jnp.where(lane == NZ - 1, rows, pltpu.roll(rows, NZ - 1, 1))
    down = jnp.where(lane == 0, rows, pltpu.roll(rows, 1, 1))
    return rows + depth_diffusion * (up - 2.0 * rows + down)


def kernel(
    phases_hbm, temp_hbm, columns_hbm, grains_hbm, angle_hbm, melt_hbm, owner_hbm, local_hbm,
    phases_out, temp_out,
    cells, cells2, static, static2, mixed, gathered, gathered2,
    temp, columns, grains, angles, melts, owners, locals_,
    req_out, req_in, rows_out, rows_in, rows_out2, rows_in2, share, share2,
    heat_out, heat_in, heat_out2, heat_in2, target_out, target_in,
    own_v, own_v2, all_v, all_v2, by_owner, flat, heat_flat, final_temp,
    load_sem, send_sem, recv_sem,
):
    tile = lax.axis_index("tile")
    group = lax.axis_index("ch")
    block = tile // BLOCK
    place = tile % BLOCK
    partner = (group + GROUPS - block) % GROUPS
    inside = partner == block

    first = partner * BLOCK
    near_tiles = [lax.rem(tile + (TILES + step - REACH), TILES) for step in range(NEAR)]
    groups = [group] + [lax.rem(group + turn, GROUPS) for turn in range(1, GROUPS)]
    near_order = [
        (offset, turn) for turn in (2, 1, 3, 0) for offset in (0, 6, 1, 5, 2, 4, 3)
    ][:-1]

    def far_index(number):
        half = (number + 1) // 2
        turn = jnp.where(number % 2 == 0, half, BLOCK - half)
        return lax.rem(place + BLOCK // 2 + turn, BLOCK)

    def far_device(index):
        return {"tile": first + index, "ch": group}

    def near_device(offset, turn):
        return {"tile": near_tiles[offset], "ch": groups[turn]}

    loads = [
        pltpu.make_async_copy(phases_hbm, cells.at[:, pl.ds(1, PX)], load_sem.at[0]),
        pltpu.make_async_copy(temp_hbm, temp, load_sem.at[1]),
        pltpu.make_async_copy(columns_hbm, columns, load_sem.at[2]),
        pltpu.make_async_copy(grains_hbm, grains, load_sem.at[3]),
        pltpu.make_async_copy(angle_hbm, angles, load_sem.at[4]),
        pltpu.make_async_copy(melt_hbm, melts, load_sem.at[5]),
        pltpu.make_async_copy(owner_hbm, owners, load_sem.at[6]),
        pltpu.make_async_copy(local_hbm, locals_, load_sem.at[7]),
    ]
    loads[2].start()

    barrier = pltpu.get_barrier_semaphore()

    def greet_far(number, _):
        pl.semaphore_signal(
            barrier, inc=1, device_id=far_device(far_index(number)), device_id_type=MESH
        )
        return 0

    lax.fori_loop(0, BLOCK - 1, greet_far, 0)

    @pl.when(jnp.logical_not(inside))
    def _():
        greet_far(BLOCK - 1, 0)

    for offset, turn in near_order:
        pl.semaphore_signal(
            barrier, inc=1, device_id=near_device(offset, turn), device_id_type=MESH
        )

    for load in loads[:2] + loads[3:]:
        load.start()
    loads[2].wait()

    wanted = jnp.broadcast_to(columns[...].astype(F32), (COLS, COLS))
    wanted_down = wanted.T
    wanted_i = wanted.astype(jnp.int32)
    wanted_down_i = wanted_down.astype(jnp.int32)
    owner_over = wanted_i // NODES
    owner_down = wanted_down_i // NODES
    local_down = (wanted_down_i % NODES).astype(F32)
    down, over = iota((COLS, COLS), 0), iota((COLS, COLS), 1)
    same = owner_over == owner_down
    slot_over = jnp.sum(jnp.where(same & (down < over), 1.0, 0.0), axis=0, keepdims=True)
    slot_down = jnp.sum(jnp.where(same & (over < down), 1.0, 0.0), axis=1, keepdims=True)
    key_over = owner_over[:1] * SLOTS + slot_over.astype(jnp.int32)
    key_down = owner_down[:, :1] * SLOTS + slot_down.astype(jnp.int32)
    ask = jnp.where(iota((FAR, COLS), 0) + partner * FAR == key_over, 1.0, 0.0).astype(BF16)
    flat[pl.ds(0, FAR), :] = dot(ask, local_down.astype(BF16))
    for index in range(BLOCK):
        req_out[index] = flat[pl.ds(index * SLOTS, SLOTS), :]
    pl.semaphore_wait(
        barrier, NEAR * GROUPS - 1 + jnp.where(inside, BLOCK - 1, BLOCK).astype(jnp.int32)
    )

    def far_copy(source, target, index, number):
        return pltpu.make_async_remote_copy(
            src_ref=source.at[index],
            dst_ref=target.at[place],
            send_sem=send_sem.at[number],
            recv_sem=recv_sem.at[number],
            device_id=far_device(index),
            device_id_type=MESH,
        )

    def far_send(source, target, number):
        def one(order, _):
            far_copy(source, target, far_index(order), number).start()
            return 0

        lax.fori_loop(0, BLOCK - 1, one, 0)

        @pl.when(jnp.logical_not(inside))
        def _():
            one(BLOCK - 1, 0)

        @pl.when(inside)
        def _():
            target[place] = source[place]

    def far_done(buffer, sem, number):
        @pl.when(inside)
        def _():
            part = buffer.at[pl.ds(0, BLOCK - 1)]
            pltpu.make_async_copy(part, part, sem.at[number]).wait()

        @pl.when(jnp.logical_not(inside))
        def _():
            pltpu.make_async_copy(buffer, buffer, sem.at[number]).wait()

    def heat_send(source, target, number):
        for offset, turn in near_order:
            pltpu.make_async_remote_copy(
                src_ref=source.at[offset],
                dst_ref=target.at[offset * GROUPS + group],
                send_sem=send_sem.at[number],
                recv_sem=recv_sem.at[number],
                device_id=near_device(offset, turn),
                device_id_type=MESH,
            ).start()
        target[REACH * GROUPS + group] = source[REACH]

    def heat_done(buffer, sem, number):
        part = buffer.at[pl.ds(0, NEAR * GROUPS - 1)]
        pltpu.make_async_copy(part, part, sem.at[number]).wait()

    def target_send(number):
        for offset in (0, 6, 1, 5, 2, 4):
            pltpu.make_async_remote_copy(
                src_ref=target_out.at[offset],
                dst_ref=target_in.at[offset],
                send_sem=send_sem.at[number],
                recv_sem=recv_sem.at[number],
                device_id=near_device(offset, 0),
                device_id_type=MESH,
            ).start()
        target_in[REACH] = target_out[REACH]

    def target_done(buffer, sem, number):
        part = buffer.at[pl.ds(0, NEAR - 1)]
        pltpu.make_async_copy(part, part, sem.at[number]).wait()

    def group_copies(source_of, target_of, number):
        return [
            pltpu.make_async_remote_copy(
                src_ref=source_of(turn),
                dst_ref=target_of(turn),
                send_sem=send_sem.at[number + turn],
                recv_sem=recv_sem.at[number + turn],
                device_id=near_device(REACH, turn),
                device_id_type=MESH,
            )
            for turn in range(1, GROUPS)
        ]

    def ring_copies(buffer, number):
        def move(owner, part, turn, order):
            piece = buffer.at[owner, pl.ds(part * QUARTER, QUARTER)]
            return pltpu.make_async_remote_copy(
                src_ref=piece,
                dst_ref=piece,
                send_sem=send_sem.at[number + order],
                recv_sem=recv_sem.at[number + order],
                device_id=near_device(REACH, turn),
                device_id_type=MESH,
            )

        right = [move(group, part, 1, part) for part in (0, 1, 2, 3)]
        left = [move(group, part, 3, 4 + part) for part in (2, 3, 0, 1)]
        starts = [copy for pair in zip(right, left) for copy in pair]
        onward = []
        for step in range(2):
            onward.append(move(groups[3], step, 1, 8 + step))
            onward.append(move(groups[1], step + 2, 3, 10 + step))
        return starts, starts[:4], onward, starts[4:] + onward

    def halo_copies(buffer, number):
        return [
            pltpu.make_async_remote_copy(
                src_ref=buffer.at[:, 1],
                dst_ref=buffer.at[:, PX + 1],
                send_sem=send_sem.at[number],
                recv_sem=recv_sem.at[number],
                device_id=near_device(REACH - 1, 0),
                device_id_type=MESH,
            ),
            pltpu.make_async_remote_copy(
                src_ref=buffer.at[:, PX],
                dst_ref=buffer.at[:, 0],
                send_sem=send_sem.at[number + 1],
                recv_sem=recv_sem.at[number + 1],
                device_id=near_device(REACH + 1, 0),
                device_id_type=MESH,
            ),
        ]

    REQ, ROWS, ROWS2, HEAT, HEAT2, TARGET = 0, 1, 2, 3, 4, 5
    HALO, HALO2 = 6, 8
    GATHER, GATHER2, SHARE, SHARE2, VEE, VEE2 = 10, 14, 26, 30, 34, 38

    far_send(req_out, req_in, REQ)

    for load in loads[:2] + loads[3:]:
        load.wait()

    key_lane = iota((COLS, FAR), 1)
    take_own = jnp.where(key_lane + partner * FAR == key_down, 1.0, 0.0).astype(BF16)
    row_all = iota((GROUPS * FAR, COLS), 0)
    row_block = ((group + row_all // FAR) % GROUPS + GROUPS - block) % GROUPS
    give_all = jnp.where(row_block * FAR + row_all % FAR == key_over, 1.0, 0.0).astype(BF16)
    give_all = tripled(give_all)
    lane_all = iota((COLS, GROUPS * FAR), 1)
    lane_group = (group + GROUPS - lane_all // FAR) % GROUPS
    lane_block = (lane_group + GROUPS - block) % GROUPS
    take_turn = jnp.where(
        lane_block * FAR + lane_all % FAR == key_down, 1.0, 0.0
    ).astype(BF16)
    take_turn = tripled(take_turn)

    row_down, lane = iota((POOL, COLS), 0), iota((POOL, COLS), 1)
    off_down = jnp.zeros((POOL, COLS), jnp.int32)
    off_over = jnp.zeros((POOL, COLS), jnp.int32)
    local_rows = jnp.zeros((POOL, NZ), jnp.int32)
    for row in range(POOL):
        off = (owners[row] - tile + (REACH + TILES)) % TILES
        off_down = jnp.where(row_down == row, off, off_down)
        off_over = jnp.where(lane // 8 == row, off, off_over)
        local_rows = jnp.where(row_down == row, locals_[row], local_rows)
    earlier = jnp.where((off_down == off_over) & (row_down < lane // 8), 1.0, 0.0)
    heat_slot = jnp.sum(earlier, axis=0, keepdims=True).astype(jnp.int32)
    heat_key = off_over[:1] * HEAT_SLOTS + heat_slot
    spread = iota((HEAT_PAD, COLS), 0) == heat_key
    pool_pick = jnp.where(spread, 1.0, 0.0).astype(BF16)
    row_of = jnp.where(iota((COLS, POOL), 0) == 8 * iota((COLS, POOL), 1), 1.0, 0.0).astype(BF16)
    row_pick = dot(pool_pick, row_of).astype(BF16)
    slot_pick = tripled(dot(pool_pick, take_own).astype(BF16))
    pool_pick = tripled(pool_pick)
    flat[pl.ds(0, HEAT_PAD), :] = dot(row_pick, local_rows.astype(F32).astype(BF16))
    for offset in range(NEAR):
        target_out[offset] = flat[pl.ds(offset * HEAT_SLOTS, HEAT_SLOTS), :]

    def first_look(channel, total):
        now = cells[channel, pl.ds(1, PX)]
        gathered[group, channel] = now.astype(BF16)
        return total + (now - now * now)

    total = lax.fori_loop(0, CH, first_look, jnp.zeros((PX, PY, NZ), F32))
    total = (time_step * drive_gain) * total.reshape(COLS, NZ)
    own_v[...] = dot(give_all, stacked(total)).reshape(GROUPS, FAR, NZ)

    warm = conduct(temp[...])
    cold_parts, warm_parts = stacked(temp[...]), stacked(warm)
    target_send(TARGET)
    halos = halo_copies(cells, HALO)
    vees = group_copies(lambda turn: own_v.at[turn], lambda turn: all_v.at[turn], VEE)
    gathers = group_copies(
        lambda turn: gathered.at[group], lambda turn: gathered.at[group], GATHER
    )
    for copy in halos + vees + gathers:
        copy.start()

    angle_down = jnp.zeros((SLOT_ALL, NZ), F32)
    angle_over = jnp.zeros((SLOT_ALL, NZ), F32)
    slot_row, slot_lane = iota((SLOT_ALL, NZ), 0), iota((SLOT_ALL, NZ), 1)
    for slot in range(SLOT_ALL):
        angle = angles[grains[slot]]
        angle_down = jnp.where(slot_row == slot, angle, angle_down)
        angle_over = jnp.where(slot_lane == slot, angle, angle_over)
    strength = interface_energy / SLOT_ALL * (0.3 + jnp.abs(jnp.sin(angle_down - angle_over)))
    strength = jnp.where((slot_row != slot_lane) & (slot_lane < SLOT_ALL), strength, 0.0)
    strength = strength.astype(BF16)
    column_sums = jnp.sum(strength.astype(F32), axis=0, keepdims=True)
    own_row = iota((COLS, SLOT_ALL), 0) // PY + group * CH
    choose = jnp.where(own_row == iota((COLS, SLOT_ALL), 1), 1.0, 0.0).astype(BF16)
    tall = dot(choose, strength).astype(BF16)
    wide_shape = (NZ, SLOT_ALL * PY)
    widen = jnp.where(iota(wide_shape, 0) == iota(wide_shape, 1) // PY, 1.0, 0.0).astype(BF16)
    weights = dot(tall, widen)
    weights = jnp.where(iota(wide_shape, 0) % PY == iota(wide_shape, 1) % PY, weights, 0.0)
    weights = weights.astype(BF16)
    for owner in range(GROUPS):
        by_owner[owner] = weights[:, owner * COLS : (owner + 1) * COLS]

    def melt_of(channel):
        return melts[grains[group * CH + channel]]

    def sum_of(channel):
        lanes = iota((1, NZ), 1) == group * CH + channel
        return jnp.sum(jnp.where(lanes, column_sums, 0.0), axis=1, keepdims=True)

    def stencil(buffer, kept):
        @pl.when(tile == 0)
        def _():
            buffer[:, 0] = jnp.zeros((CH, PY, NZ), F32)

        @pl.when(tile == TILES - 1)
        def _():
            buffer[:, PX + 1] = jnp.zeros((CH, PY, NZ), F32)

        def one(channel, total):
            padded = buffer[channel]
            now = padded[1:-1].reshape(COLS, NZ)
            gain = time_step * laplacian(padded)
            gain = gain + (melt_of(channel) * (time_step * drive_gain)) * (now - now * now)
            kept[channel] = now + gain
            rounded = now.astype(BF16).astype(F32)
            return total + (gain - (time_step * sum_of(channel)) * rounded)

        return lax.fori_loop(0, CH, one, jnp.zeros((COLS, NZ), F32))

    def mix(buffer):
        for plane in range(PX):
            right = buffer[:, :, plane].reshape(SLOT_ALL * PY, NZ)
            mixed[:, plane] = dot(weights, right).reshape(CH, PY, NZ)

    for copy in halos:
        copy.wait_recv()
    own_u = stencil(cells, static)

    far_done(req_in, recv_sem, REQ)
    for index in range(BLOCK):
        flat[pl.ds(index * SLOTS, SLOTS), :] = req_in[index]
    asked = flat[pl.ds(0, FAR), :].astype(jnp.int32)
    asked = jnp.concatenate([asked, asked], axis=1)
    serve = jnp.where(asked == iota((FAR, NODES), 1), 1.0, 0.0).astype(BF16)

    def spread_rows(values, out):
        flat[pl.ds(0, FAR), :] = values
        for index in range(BLOCK):
            out[index] = flat[pl.ds(index * SLOTS, SLOTS), :]

    def collect_rows(buffer, kept):
        for index in range(BLOCK):
            kept[0, pl.ds(index * SLOTS, SLOTS), :] = buffer[index]

    serve = tripled(serve)
    spread_rows(dot(serve, cold_parts), rows_out)
    far_send(rows_out, rows_in, ROWS)

    target_done(target_in, recv_sem, TARGET)
    heat_flat[...] = jnp.full((HEAT_PAD, NZ), -1.0, F32)
    for offset in range(NEAR):
        heat_flat[pl.ds(offset * HEAT_SLOTS, HEAT_SLOTS), :] = target_in[offset]
    aims = heat_flat[...].astype(jnp.int32)
    aims = jnp.concatenate([aims, jnp.full((NZ - HEAT_PAD, NZ), -1, jnp.int32)], axis=0)
    low = jnp.where(aims == iota((NZ, NZ), 1), 1.0, 0.0).T
    high = jnp.where(aims == iota((NZ, NZ), 1) + NZ, 1.0, 0.0).T
    scatter = jnp.concatenate([low, high], axis=0)[:, :HEAT_PAD].astype(BF16)
    relay = tripled(dot(serve[:, :NODES], scatter).astype(BF16))
    scatter = tripled(scatter)
    warm_rows = dot(serve, warm_parts)
    heat_flat[...] = jnp.zeros((HEAT_PAD, NZ), F32)

    def arrived_heat(buffer):
        for offset in range(NEAR):
            parts = [buffer[offset * GROUPS + turn] for turn in range(GROUPS)]
            heat_flat[pl.ds(offset * HEAT_SLOTS, HEAT_SLOTS), :] = (parts[0] + parts[1]) + (
                parts[2] + parts[3]
            )
        return heat_flat[...]

    def send_heat(kept, own_part, vee, out, target, number):
        warmed = dot(slot_pick, stacked(kept[0] * vee))
        flat[pl.ds(0, HEAT_PAD), :] = own_part - warmed
        for offset in range(NEAR):
            out[offset] = flat[pl.ds(offset * HEAT_SLOTS, HEAT_SLOTS), :]
        heat_send(out, target, number)

    def share_copies(buffer, number):
        return group_copies(lambda turn: buffer.at[0], lambda turn: buffer.at[turn], number)

    for copy in vees:
        copy.wait_recv()
    vee = (own_v[0] + all_v[1]) + (all_v[2] + all_v[3])
    fixed_heat = dot(pool_pick, stacked(own_u))

    far_done(rows_in, recv_sem, ROWS)
    collect_rows(rows_in, share)
    shares = share_copies(share, SHARE)
    for copy in shares:
        copy.start()
    send_heat(share, fixed_heat, vee, heat_out, heat_in, HEAT)
    for copy in gathers:
        copy.wait_recv()
    mix(gathered)
    for copy in shares:
        copy.wait_recv()

    def all_rows(kept):
        return dot(take_turn, stacked(kept[...].reshape(GROUPS * FAR, NZ)))

    cell_temp = all_rows(share)

    def update(channel, total):
        now = cells[channel, pl.ds(1, PX)].reshape(COLS, NZ)
        change = (time_step * drive_gain) * cell_temp * (now - now * now)
        mixing = mixed[channel].reshape(COLS, NZ)
        new = static[channel] - time_step * mixing - change
        shaped = new.reshape(PX, PY, NZ)
        cells2[channel, pl.ds(1, PX)] = shaped
        gathered2[group, channel] = shaped.astype(BF16)
        return total + (new - new * new)

    total = lax.fori_loop(0, CH, update, jnp.zeros((COLS, NZ), F32))
    ring2 = ring_copies(gathered2, GATHER2)
    for copy in ring2[0][:4]:
        copy.start()
    total = (time_step * drive_gain) * total
    own_v2[...] = dot(give_all, stacked(total)).reshape(GROUPS, FAR, NZ)
    halos2 = halo_copies(cells2, HALO2)
    vees2 = group_copies(lambda turn: own_v2.at[turn], lambda turn: all_v2.at[turn], VEE2)
    for copy in vees2 + halos2 + ring2[0][4:]:
        copy.start()

    heat_done(heat_in, recv_sem, HEAT)
    arrived = arrived_heat(heat_in)
    spread_rows(warm_rows + heat_gain * dot(relay, stacked(arrived)), rows_out2)
    far_send(rows_out2, rows_in2, ROWS2)
    final_temp[...] = conduct(warm + heat_gain * dot(scatter, stacked(arrived)))

    for copy in halos2:
        copy.wait_recv()
    for arrived_copy, onward in zip(ring2[1], ring2[2]):
        arrived_copy.wait_recv()
        onward.start()
    own_u2 = stencil(cells2, static2)
    for copy in vees2:
        copy.wait_recv()
    vee2 = (own_v2[0] + all_v2[1]) + (all_v2[2] + all_v2[3])
    fixed_heat2 = dot(pool_pick, stacked(own_u2))

    far_done(rows_in2, recv_sem, ROWS2)
    collect_rows(rows_in2, share2)
    send_heat(share2, fixed_heat2, vee2, heat_out2, heat_in2, HEAT2)
    shares2 = share_copies(share2, SHARE2)
    for copy in shares2:
        copy.start()

    for copy in ring2[3][:4]:
        copy.wait_recv()

    def block_of(owner, plane):
        right = gathered2[owner, :, plane].reshape(COLS, NZ)
        return dot(by_owner[owner], right).reshape(CH, PY, NZ)

    for plane in range(PX):
        mixed[:, plane] = block_of(group, plane) + (
            block_of(groups[1], plane) + block_of(groups[3], plane)
        )
    for copy in ring2[3][4:]:
        copy.wait_recv()
    for plane in range(PX):
        mixed[:, plane] += block_of(groups[2], plane)
    for copy in shares2:
        copy.wait_recv()
    cell_temp2 = all_rows(share2)

    stores = []
    for channel in range(CH):
        now = cells2[channel, pl.ds(1, PX)].reshape(COLS, NZ)
        change = (time_step * drive_gain) * cell_temp2 * (now - now * now)
        mixing = mixed[channel].reshape(COLS, NZ)
        static2[channel] = static2[channel] - time_step * mixing - change
        store = pltpu.make_async_copy(
            static2.at[channel], phases_out.at[channel], load_sem.at[channel]
        )
        store.start()
        stores.append(store)

    heat_done(heat_in2, recv_sem, HEAT2)
    arrived = arrived_heat(heat_in2)
    final_temp[...] = final_temp[...] + heat_gain * dot(scatter, stacked(arrived))
    store_temp = pltpu.make_async_copy(final_temp, temp_out, load_sem.at[CH])
    store_temp.start()

    far_done(req_out, send_sem, REQ)
    far_done(rows_out, send_sem, ROWS)
    far_done(rows_out2, send_sem, ROWS2)
    heat_done(heat_in, send_sem, HEAT)
    heat_done(heat_in2, send_sem, HEAT2)
    target_done(target_out, send_sem, TARGET)
    for copy in halos + vees + gathers + shares + halos2 + vees2 + ring2[0] + ring2[2] + shares2:
        copy.wait_send()
    for store in stores + [store_temp]:
        store.wait()


def place_results(new, temp, new_out, temp_out):
    new_out[...] = new[...]
    temp_out[...] = temp[...]


def on_device(
    phases, node_temp, column_nodes, grain_ids, grain_angle, grain_melt, heat_owner, heat_local
):
    outside = pl.BlockSpec(memory_space=pl.ANY)
    vmem, smem = pltpu.VMEM, pltpu.SMEM
    gathered = vmem((GROUPS, CH, PX, PY, NZ), BF16)
    padded = vmem((CH, PX + 2, PY, NZ), F32)
    flat_cells = vmem((CH, COLS, NZ), F32)
    mix_out = vmem((CH, PX, PY, NZ), F32)
    far_rows = vmem((BLOCK, SLOTS, NZ), F32)
    shared = vmem((GROUPS, FAR, NZ), F32)
    heat_out = vmem((NEAR, HEAT_SLOTS, NZ), F32)
    heat_in = vmem((NEAR * GROUPS, HEAT_SLOTS, NZ), F32)
    new, temp = pl.pallas_call(
        kernel,
        out_shape=(
            jax.ShapeDtypeStruct((CH, COLS, NZ), F32),
            jax.ShapeDtypeStruct(node_temp.shape, F32),
        ),
        in_specs=[outside] * 8,
        out_specs=(outside, outside),
        scratch_shapes=[
            padded, padded, flat_cells, flat_cells, mix_out, gathered, gathered,
            vmem((NODES, NZ), F32), vmem((1, COLS), jnp.int32), smem((SLOT_ALL,), jnp.int32),
            smem((grain_angle.shape[0],), F32), smem((grain_melt.shape[0],), F32),
            smem((POOL,), jnp.int32), smem((POOL,), jnp.int32),
            far_rows, far_rows, far_rows, far_rows, far_rows, far_rows, shared, shared,
            heat_out, heat_in, heat_out, heat_in, heat_out, heat_out,
            shared, shared, shared, shared, vmem((GROUPS, COLS, COLS), BF16), vmem((FAR, NZ), F32), vmem((HEAT_PAD, NZ), F32),
            vmem((NODES, NZ), F32),
            pltpu.SemaphoreType.DMA((CH + 1,)),
            pltpu.SemaphoreType.DMA((42,)),
            pltpu.SemaphoreType.DMA((42,)),
        ],
        compiler_params=pltpu.CompilerParams(
            collective_id=0, has_side_effects=True, vmem_limit_bytes=56 << 20
        ),
        name="solidify",
    )(
        phases,
        node_temp,
        column_nodes.reshape(1, COLS),
        grain_ids.reshape(SLOT_ALL),
        grain_angle,
        grain_melt,
        heat_owner.reshape(POOL),
        heat_local,
    )
    halves = (
        pl.BlockSpec((CH // 2, COLS, NZ), lambda half: (half, 0, 0)),
        pl.BlockSpec((NODES // 2, NZ), lambda half: (half, 0)),
    )
    placed, temp = pl.pallas_call(
        place_results,
        out_shape=(
            jax.ShapeDtypeStruct(new.shape, F32),
            jax.ShapeDtypeStruct(temp.shape, F32),
        ),
        grid=(2,),
        in_specs=halves,
        out_specs=halves,
        name="results",
    )(new, temp)
    return placed.reshape(phases.shape), temp


def solution(mesh):
    placed = (
        P("ch", "tile", None, None),
        P("tile", None),
        P("tile"),
        P("tile", None),
        P(),
        P(),
        P("tile", None),
        P("tile"),
    )
    return jax.shard_map(
        on_device,
        mesh=mesh,
        in_specs=placed,
        out_specs=(P("ch", "tile", None, None), P("tile", None)),
        check_vma=False,
    )
```
